32 devices in a mesh: parts: 2 (over x), tm: 16 (over z, y, core).
Axes of the slice: x: 2, y: 2, z: 4, core: 2. Of those that a mesh axis runs over, the one named last changes fastest.
Arguments:
- initial: float32 [16, 6, 16, 2048], P('tm', 'parts'), parts along dimension 1, may hold values from -0.6 to 0.6
- velocity: float32 [128, 4, 16, 2048], P('tm', 'parts'), parts along dimension 1, may hold values from -3 to 3
- forcing: float32 [128, 32, 2048], P('tm', 'parts'), parts along dimension 1, may hold values from -0.3 to 0.3
- depth_table: float32 [16], replicated, may hold values from 0.3 to 1.2
- levels: int32 [32, 2048], P('parts'), parts along dimension 0, may hold values from 0 to 15
- wet_mask: int32 [32, 2048], P('parts'), parts along dimension 0, may hold values 0 or 1
Outputs:
- corrected: float32 [16, 6, 16, 2048], P('tm', 'parts'), parts along dimension 1
- gradient: float32 [32, 2048], P('parts'), parts along dimension 0
The draws below stay inside these ranges and needn't reach their ends.
There are 2 independent parts, one for each index of `parts`. The reference program is written for one: setup_inputs(seed, part) draws one part's arguments, and reference() takes and returns one part's arrays. A program takes and returns all parts, laid end to end along the dimension named above; an argument that names none is the same for every part. Nothing has to cross between parts.
All inputs are finite; a program needn't handle non-finite values.
Results may differ from the reference program's by a relative error of at most 0.00002.
Values sent between devices are 32-bit elements; how exact they have to be, the bound alone decides.
No kernel may reach another device: no remote copies, remote signals or barrier semaphores. Data moves between devices by JAX's collectives and lax.ppermute only.
A program may use at most 128 MiB of HBM per device.

```python
import math
import jax
import jax.numpy as jnp
from jax import lax

ROWS = 16
COLS = 2048
FINE = 8
LEVELS = 16
SLICES = 16
STEPS = 128


def place_ends(drawn, stream_key, low, top_value):
    dims = drawn.shape
    place = [jax.random.randint(jax.random.fold_in(stream_key, axis), (), 0, dims[axis]) for axis in range(len(dims))]
    drawn = drawn.at[tuple(place)].set(low)
    longest = dims.index(max(dims))
    place[longest] = (place[longest] + 1) % dims[longest]
    return drawn.at[tuple(place)].set(top_value)


def block_levels(stream_key, dims, shards, least, top_value):
    loudness = 1.0
    for axis_at, shards_of in shards:
        draws = jax.random.uniform(jax.random.fold_in(jax.random.fold_in(stream_key, 6), axis_at), (shards_of,), jnp.float32, least / len(shards), top_value / len(shards))
        loudness = loudness * jnp.repeat(jnp.exp(draws), dims[axis_at] // shards_of).reshape((-1,) + (1,) * (len(dims) - 1 - axis_at))
    return loudness


def bell_draw(rng, extent, spread, reach, shards=(), kind=jnp.bfloat16):
    entries = spread * jax.random.normal(rng, extent, jnp.float32)
    if shards:
        entries = entries * block_levels(rng, extent, shards, -0.22, 0.18)
    return jnp.clip(entries, -reach, reach).astype(kind)


def setup_inputs(seed: int = 0, part: int = 0) -> dict:
    keys = jax.random.split(jax.random.key(seed), 7)
    own_keys = jax.random.split(jax.random.fold_in(keys[6], part), 7)
    initial = bell_draw(own_keys[0], (SLICES, 3, ROWS, COLS), 0.1, 0.6, ((0, 16),), jnp.float32)
    velocity = bell_draw(own_keys[1], (STEPS, 2, ROWS, COLS), 0.5, 3.0, ((0, 16),), jnp.float32)
    forcing = bell_draw(own_keys[2], (STEPS, ROWS, COLS), 0.05, 0.3, ((0, 16),), jnp.float32)
    depth_table = jnp.clip(jnp.exp(jax.random.uniform(keys[3], (LEVELS,), jnp.float32, math.log(0.3), math.log(1.2))), 0.3, 1.2)
    levels = place_ends(jax.random.randint(own_keys[4], (ROWS, COLS), 0, LEVELS), jax.random.fold_in(own_keys[4], 1), 0, LEVELS - 1).astype(jnp.int32)
    wet_mask = place_ends((jax.random.randint(own_keys[5], (ROWS, COLS), 0, 4) < 3).astype(jnp.int32), jax.random.fold_in(own_keys[5], 1), 0, 1)
    return dict(initial=initial, velocity=velocity, forcing=forcing, depth_table=depth_table, levels=levels, wet_mask=wet_mask)


COURANT = 0.06

def face_depths(depths):
    face_x = jnp.pad(0.5 * (depths[:, :-1] + depths[:, 1:]), ((0, 0), (0, 1)))
    face_y = jnp.pad(0.5 * (depths[:-1, :] + depths[1:, :]), ((0, 1), (0, 0)))
    return (face_x, face_y)

def divergence(flux_x, flux_y):
    west = jnp.pad(flux_x[:, :-1], ((0, 0), (1, 0)))
    south = jnp.pad(flux_y[:-1, :], ((1, 0), (0, 0)))
    return flux_x - west + flux_y - south

def forward_step(fields, face_x, face_y, courant):
    surface = fields[0]
    slope_x = jnp.pad(surface[:, 1:] - surface[:, :-1], ((0, 0), (0, 1)))
    slope_y = jnp.pad(surface[1:, :] - surface[:-1, :], ((0, 1), (0, 0)))
    east_flow = fields[1] - courant * slope_x
    north_flow = fields[2] - courant * slope_y
    surface_new = surface - courant * divergence(face_x * east_flow, face_y * north_flow)
    return jnp.stack([surface_new, east_flow, north_flow])

def adjoint_step(adjoint, face_x, face_y, courant):
    unused, pullback = jax.vjp(lambda fields: forward_step(fields, face_x, face_y, courant), adjoint)
    return pullback(adjoint)[0]

def depth_pull(cell_depth, flow_pair, surface_adjoint):

    def flux_term(depths):
        face_x, face_y = face_depths(depths)
        return -COURANT * divergence(face_x * flow_pair[0], face_y * flow_pair[1])
    unused, pullback = jax.vjp(flux_term, cell_depth)
    return pullback(surface_adjoint)[0]

def sweep(start, forcing, velocity, cell_depth, face_x, face_y, with_grad):
    adjoint = start
    partial_grad = jnp.zeros(cell_depth.shape, jnp.float32)
    for step_no in reversed(range(velocity.shape[0])):
        if with_grad:
            partial_grad = partial_grad + depth_pull(cell_depth, velocity[step_no], adjoint[0])
        adjoint = adjoint_step(adjoint, face_x, face_y, COURANT)
        if forcing is not None:
            adjoint = adjoint.at[0].add(forcing[step_no])
    return (adjoint, partial_grad)

def restrict(field):
    shaped = field.reshape(field.shape[:-2] + (field.shape[-2] // 2, 2, field.shape[-1] // 2, 2))
    return shaped.mean(axis=(-3, -1))

def prolong(field):
    return jnp.repeat(jnp.repeat(field, 2, axis=-2), 2, axis=-1)

def level_depth(depth_table, levels, wet_mask):
    selector = (levels[..., None] == jnp.arange(depth_table.shape[0], dtype=jnp.int32)).astype(jnp.float32)
    return wet_mask.astype(jnp.float32) * lax.optimization_barrier(jnp.sum(selector * depth_table, axis=-1))

def reference(initial, velocity, forcing, depth_table, levels, wet_mask):
    cell_depth = level_depth(depth_table, levels, wet_mask)
    face_x, face_y = face_depths(cell_depth)
    coarse_x, coarse_y = face_depths(restrict(cell_depth))
    coarse_courant = FINE * COURANT / 2
    forcing_slices = forcing.reshape(SLICES, FINE, ROWS, COLS)
    flow_slices = velocity.reshape(SLICES, FINE, 2, ROWS, COLS)
    following = jnp.concatenate([initial[1:], jnp.zeros_like(initial[:1])])

    def relax_slice(slice_items):
        return sweep(slice_items[0], slice_items[1], slice_items[2], cell_depth, face_x, face_y, False)[0]
    relaxed = lax.map(relax_slice, (following, forcing_slices, flow_slices))
    coarse_residual = restrict(relaxed - initial)

    def backward_link(carried, residual_term):
        linked = residual_term + adjoint_step(carried, coarse_x, coarse_y, coarse_courant)
        return (linked, linked)
    unused, correction = lax.scan(backward_link, jnp.zeros_like(coarse_residual[0]), coarse_residual, reverse=True)
    corrected = initial + prolong(correction)
    following = jnp.concatenate([corrected[1:], jnp.zeros_like(corrected[:1])])

    def slice_gradient(slice_items):
        return sweep(slice_items[0], slice_items[1], slice_items[2], cell_depth, face_x, face_y, True)[1]
    partials = lax.map(slice_gradient, (following, forcing_slices, flow_slices))
    summed = lax.optimization_barrier(jnp.sum(partials, axis=0))
    return (corrected, wet_mask.astype(jnp.float32) * summed)
```

```python
import functools

import jax
import jax.numpy as jnp
from jax import lax
from jax.experimental import pallas as pl
from jax.experimental.pallas import tpu as pltpu
from jax.sharding import PartitionSpec as P

COURANT = 0.06
LANES = 128
VMEM = pl.BlockSpec(memory_space=pltpu.VMEM)
SMEM = pl.BlockSpec(memory_space=pltpu.SMEM)
EXACT = lax.Precision.HIGHEST


def roll(value, steps, axis):
    return pltpu.roll(value, steps % value.shape[axis], axis)


def index_of(shape, axis):
    return lax.broadcasted_iota(jnp.int32, shape, axis)


def faces(depth, scale):
    rows, cols = depth.shape
    half = 0.5 * scale
    east = half * (depth + roll(depth, -1, 1))
    north = half * (depth + roll(depth, -1, 0))
    east = jnp.where(index_of(depth.shape, 1) < cols - 1, east, 0.0)
    north = jnp.where(index_of(depth.shape, 0) < rows - 1, north, 0.0)
    return east, north


def fine_step(s, e, n, face_x, face_y):
    slope_x = roll(s, -1, 1) - s
    slope_y = roll(s, -1, 0) - s
    e = e + face_x * slope_x
    n = n + face_y * slope_y
    s = s + ((e - roll(e, 1, 1)) + (n - roll(n, 1, 0)))
    return s, e, n, slope_x, slope_y


def coarse_step(fields, face_x, face_y):
    s, e, n = fields
    rows, cols = s.shape
    e = e + face_x * (roll(s, -1, 1) - s)
    n = n + face_y * (roll(s, -1, 0) - s)
    e_in = jnp.where(index_of(s.shape, 1) < cols - 1, e, 0.0)
    n_in = jnp.where(index_of(s.shape, 0) < rows - 1, n, 0.0)
    s = s + ((e_in - roll(e_in, 1, 1)) + (n_in - roll(n_in, 1, 0)))
    return s, e, n


def power(fields, count, face_x, face_y):
    if count <= 4:
        for _ in range(count):
            fields = coarse_step(fields, face_x, face_y)
        return fields
    return lax.fori_loop(0, count, lambda _, f: coarse_step(f, face_x, face_y), fields)


def add(a, b):
    return tuple(x + y for x, y in zip(a, b))


def scaled(a, factor):
    return tuple(x * factor for x in a)


def pick(first, a, b):
    return tuple(jnp.where(first, x, y) for x, y in zip(a, b))


def read(ref, at=0):
    return tuple(ref[at + i] for i in range(3))


def write(ref, fields, at=0):
    for i, field in enumerate(fields):
        ref[at + i] = field


def pair_matrix(shape, wide_axis, weight):
    wide = index_of(shape, wide_axis) // 2
    return jnp.where(wide == index_of(shape, 1 - wide_axis), weight, 0.0)


def product(a, b):
    return jnp.dot(a, b, precision=EXACT, preferred_element_type=jnp.float32)


def restrict_all(fields):
    rows, cols = fields[0].shape
    half = rows // 2
    stacked = jnp.concatenate(fields, axis=0)
    gather = pair_matrix((2 * LANES, LANES), 0, 0.25)
    merged = jnp.concatenate(
        [product(stacked[:, c : c + 2 * LANES], gather) for c in range(0, cols, 2 * LANES)], axis=1
    )
    merged = product(pair_matrix((stacked.shape[0] // 2, stacked.shape[0]), 1, 1.0), merged)
    return [merged[i * half : (i + 1) * half] for i in range(len(fields))]


def prolong_all(fields):
    half, cols = fields[0].shape
    stacked = jnp.concatenate(fields, axis=0)
    stacked = product(pair_matrix((2 * stacked.shape[0], stacked.shape[0]), 0, 1.0), stacked)
    spread = pair_matrix((LANES, 2 * LANES), 1, 1.0)
    merged = jnp.concatenate(
        [product(stacked[:, c : c + LANES], spread) for c in range(0, cols, LANES)], axis=1
    )
    return [merged[2 * i * half : 2 * (i + 1) * half] for i in range(len(fields))]


def prepare(table, levels, wet, initial, forcing, own, sent, fine_faces, coarse_faces):
    rows, cols = levels.shape
    steps = forcing.shape[0]
    width = own.shape[2]
    coarse_cols = cols // 2
    level = levels[...]
    depth = jnp.zeros((rows, cols), jnp.float32)
    for i in range(table.shape[0]):
        depth = jnp.where(level == i, table[i], depth)
    depth = depth * wet[...].astype(jnp.float32)
    face_x, face_y = faces(depth, COURANT * COURANT)
    fine_faces[0] = face_x
    fine_faces[1] = face_y
    inner_x = index_of((rows, cols), 1) < cols - 1
    inner_y = index_of((rows, cols), 0) < rows - 1

    s0, e0, n0 = initial[0, 0], initial[0, 1] * COURANT, initial[0, 2] * COURANT
    s, e, n = s0, jnp.where(inner_x, e0, 0.0), jnp.where(inner_y, n0, 0.0)
    for _ in range(steps):
        s, e, n, _, _ = fine_step(s, e, n, face_x, face_y)
    relaxed = [s, jnp.where(inner_x, e, e0), jnp.where(inner_y, n, n0)]

    s = forcing[steps - 1]
    e = jnp.zeros_like(s)
    n = jnp.zeros_like(s)
    for step in reversed(range(steps - 1)):
        s, e, n, _, _ = fine_step(s, e, n, face_x, face_y)
        s = s + forcing[step]
    relaxed += [s - s0, e - e0, n - n0, depth]
    su, eu, nu, sw, ew, nw, coarse_depth = restrict_all(relaxed)
    ratio = steps / 2
    coarse_courant = COURANT * ratio
    cx, cy = faces(coarse_depth, coarse_courant * coarse_courant)
    w = (sw, ew * ratio, nw * ratio)
    g = add((su, eu * ratio, nu * ratio), coarse_step(w, cx, cy))

    core = lax.rem(lax.axis_index("tm"), 2)
    right = coarse_cols - width

    def store(mine, other):
        for ref, at in ((own, mine), (sent, other)):
            for i in range(3):
                ref[i] = g[i][:, at : at + width]
                ref[3 + i] = w[i][:, at : at + width]
        coarse_faces[0] = cx[:, mine : mine + width]
        coarse_faces[1] = cy[:, mine : mine + width]

    @pl.when(core == 0)
    def _():
        store(0, right)

    @pl.when(core == 1)
    def _():
        store(right, 0)


def chip_pair(own, got, coarse_faces, out):
    cx, cy = coarse_faces[0], coarse_faces[1]
    first = lax.rem(lax.axis_index("tm"), 2) == 0
    g_own, g_got = read(own), read(got)
    g_low, g_high = pick(first, g_own, g_got), pick(first, g_got, g_own)
    w_low = pick(first, read(own, 3), read(got, 3))
    write(out, add(g_low, coarse_step(g_high, cx, cy)))
    write(out, add(w_low, g_high), 3)


def row_pair(own, got, coarse_faces, out, out_t):
    cx, cy = coarse_faces[0], coarse_faces[1]
    first = lax.rem(lax.axis_index("tm") // 2, 2) == 0
    t_own, t_got = read(own), read(got)
    t_low, t_high = pick(first, t_own, t_got), pick(first, t_got, t_own)
    q_low = pick(first, read(own, 3), read(got, 3))
    moved = coarse_step(t_high, cx, cy)
    total = add(t_low, coarse_step(moved, cx, cy))
    write(out, total)
    write(out_t, total)
    write(out, add(q_low, moved), 3)


def widen(stride, own, got, coarse_faces, out, *, per_row, rows_in_all):
    row = lax.axis_index("tm") // per_row
    there = jnp.where(row + stride < rows_in_all, 1.0, 0.0)
    moved = power(scaled(read(got), there), per_row * stride, coarse_faces[0], coarse_faces[1])
    write(out, add(read(own), moved))


def finish(near, far, farther, own, got, chip, partner, coarse_faces, kept, sent, *, per_row, rows_in_all):
    cx, cy = coarse_faces[0], coarse_faces[1]
    width = coarse_faces.shape[2]
    half = kept.shape[2]
    device = lax.axis_index("tm")
    row = device // per_row

    def there(stride):
        return jnp.where(row + stride < rows_in_all, 1.0, 0.0)

    rest = scaled(read(far), there(2))
    if farther is not None:
        rest = add(rest, power(scaled(read(farther), there(3)), per_row, cx, cy))
    rest = power(rest, per_row - 1, cx, cy)
    after = add(scaled(read(near, 3), there(1)), rest)
    end = add(scaled(read(near), there(1)), coarse_step(rest, cx, cy))
    if partner is not None:
        low = lax.rem(device // 2, 2) == 0
        moved = coarse_step(end, cx, cy)
        after = pick(low, add(read(partner, 3), moved), after)
        end = pick(low, add(read(partner), coarse_step(moved, cx, cy)), end)
    first = lax.rem(device, 2) == 0
    w_high = pick(first, read(got, 3), read(own, 3))
    q = read(chip, 3)
    c_low = add(q, coarse_step(end, cx, cy))
    c_high = add(w_high, end)

    @pl.when(first)
    def _():
        for i in range(3):
            kept[i] = c_low[i][:, :half]
            kept[3 + i] = c_high[i][:, :half]
            sent[i] = c_high[i][:, :half]
            sent[3 + i] = after[i][:, :half]

    @pl.when(jnp.logical_not(first))
    def _():
        for i in range(3):
            kept[i] = c_high[i][:, width - half :]
            kept[3 + i] = after[i][:, width - half :]
            sent[i] = c_low[i][:, width - half :]
            sent[3 + i] = c_high[i][:, width - half :]


def descend(kept, got, initial, following, forcing, velocity, fine_faces, wet, corrected, mine, other):
    steps = forcing.shape[0]
    rows, cols = wet.shape
    device = lax.axis_index("tm")
    first = lax.rem(device, 2) == 0
    unscale = 1.0 / (COURANT * (steps / 2))
    fields = []
    for i in range(6):
        left = jnp.where(first, kept[i], got[i])
        right = jnp.where(first, got[i], kept[i])
        field = jnp.concatenate([left, right], axis=1)
        fields.append(field if i % 3 == 0 else field * unscale)
    fields = prolong_all(fields)
    for i in range(3):
        corrected[0, i] = initial[0, i] + fields[i]

    there = jnp.where(device + 1 < lax.axis_size("tm"), 1.0, 0.0)
    inner_x = index_of((rows, cols), 1) < cols - 1
    inner_y = index_of((rows, cols), 0) < rows - 1
    s = (following[0, 0] * there) + fields[3]
    e = jnp.where(inner_x, (following[0, 1] * there + fields[4]) * COURANT, 0.0)
    n = jnp.where(inner_y, (following[0, 2] * there + fields[5]) * COURANT, 0.0)
    face_x, face_y = fine_faces[0], fine_faces[1]
    grad_x = jnp.zeros_like(s)
    grad_y = jnp.zeros_like(s)
    for step in reversed(range(steps)):
        s, e, n, slope_x, slope_y = fine_step(s, e, n, face_x, face_y)
        grad_x = grad_x + slope_x * velocity[step, 0]
        grad_y = grad_y + slope_y * velocity[step, 1]
        s = s + forcing[step]
    grad_x = jnp.where(inner_x, grad_x, 0.0)
    grad_y = jnp.where(inner_y, grad_y, 0.0)
    grad = (grad_x + roll(grad_x, 1, 1)) + (grad_y + roll(grad_y, 1, 0))
    grad = (0.5 * COURANT) * grad * wet[...].astype(jnp.float32)
    half = cols // 2

    @pl.when(first)
    def _():
        mine[...] = grad[:, :half]
        other[...] = grad[:, half:]

    @pl.when(jnp.logical_not(first))
    def _():
        mine[...] = grad[:, half:]
        other[...] = grad[:, :half]


def call(body, shapes, operands, specs=None):
    return pl.pallas_call(
        body,
        out_shape=[jax.ShapeDtypeStruct(shape, jnp.float32) for shape in shapes],
        in_specs=specs or [VMEM] * len(operands),
        out_specs=[VMEM] * len(shapes),
        compiler_params=pltpu.CompilerParams(vmem_limit_bytes=32 * 1024 * 1024),
    )(*operands)


def shards(initial, velocity, forcing, depth_table, levels, wet_mask):
    count = lax.axis_size("tm")
    rows, cols = levels.shape
    half_rows, half = rows // 2, cols // 4
    halo = -(-count // LANES) * LANES
    width = half + halo
    block = (half_rows, width)

    def paired(value, stride):
        return lax.ppermute(value, "tm", [(s, s ^ stride) for s in range(count)])

    def back(value, stride):
        return lax.ppermute(value, "tm", [(s, (s - stride) % count) for s in range(count)])

    following = lax.ppermute(initial, "tm", [(s, s - 1) for s in range(1, count)])
    own, sent, fine_faces, coarse_faces = call(
        prepare,
        [(6, *block), (6, *block), (2, rows, cols), (2, *block)],
        [depth_table, levels, wet_mask, initial, forcing],
        specs=[SMEM] + [VMEM] * 4,
    )
    got = paired(sent, 1)
    (chip,) = call(chip_pair, [(6, *block)], [own, got, coarse_faces])
    per_row = 4 if count <= 16 else 2
    rows_in_all = count // per_row
    if per_row == 4:
        partner = paired(chip, 2)
        row, row_t = call(row_pair, [(6, *block), (3, *block)], [chip, partner, coarse_faces])
    else:
        partner = None
        row, row_t = chip, chip[:3]
    near = back(row, per_row)
    if rows_in_all <= 4:
        far, farther = back(row_t, 2 * per_row), back(row_t, 3 * per_row)
    else:
        stride = 1
        while stride < rows_in_all - 2:
            (row_t,) = call(
                functools.partial(widen, stride, per_row=per_row, rows_in_all=rows_in_all),
                [(3, *block)],
                [row_t, back(row_t, stride * per_row), coarse_faces],
            )
            stride *= 2
        far, farther = back(row_t, 2 * per_row), None

    operands = {
        "near": near,
        "far": far,
        "farther": farther,
        "own": own,
        "got": got,
        "chip": chip,
        "partner": partner,
        "coarse_faces": coarse_faces,
    }
    names = [name for name, value in operands.items() if value is not None]

    def finish_body(*refs):
        given = dict.fromkeys(operands)
        given.update(zip(names, refs))
        kept, sent = refs[len(names) :]
        finish(**given, kept=kept, sent=sent, per_row=per_row, rows_in_all=rows_in_all)

    kept, sent = call(finish_body, [(6, half_rows, half)] * 2, [operands[name] for name in names])
    got = paired(sent, 1)
    corrected, mine, other = call(
        descend,
        [initial.shape, (rows, cols // 2), (rows, cols // 2)],
        [kept, got, initial, following, forcing, velocity, fine_faces, wet_mask],
    )
    mine = mine + paired(other, 1)
    if per_row == 4:
        mine = mine + paired(mine, 2)
    if rows_in_all == 4:
        mine = mine + paired(mine, 4) + paired(mine, 8) + paired(mine, 12)
    else:
        stride = per_row
        while stride < count:
            mine = mine + paired(mine, stride)
            stride *= 2
    other = paired(mine, 1)
    first = lax.rem(lax.axis_index("tm"), 2) == 0
    left, right = jnp.where(first, mine, other), jnp.where(first, other, mine)
    return corrected, jnp.concatenate([left, right], axis=1)


def solution(mesh):
    in_specs = (
        P("tm", "parts", None, None),
        P("tm", "parts", None, None),
        P("tm", "parts", None),
        P(),
        P("parts", None),
        P("parts", None),
    )
    out_specs = (P("tm", "parts", None, None), P("parts", None))
    return jax.shard_map(shards, mesh=mesh, in_specs=in_specs, out_specs=out_specs, check_vma=False)
```

```python
import functools

import jax
import jax.numpy as jnp
from jax import lax
from jax.experimental import pallas as pl
from jax.experimental.pallas import tpu as pltpu
from jax.sharding import PartitionSpec as P

COURANT = 0.06
LANES = 128
VMEM = pl.BlockSpec(memory_space=pltpu.VMEM)
HBM = pl.BlockSpec(memory_space=pltpu.HBM)
ANY = pl.BlockSpec(memory_space=pl.ANY)
PREPARE_COST = 40_000_000
BASE_COST = 8_000_000
CORRECT_COST = 4_000_000
EXACT = lax.Precision.HIGHEST


def roll(value, steps, axis):
    return pltpu.roll(value, steps % value.shape[axis], axis)


def index_of(shape, axis):
    return lax.broadcasted_iota(jnp.int32, shape, axis)


def faces(depth, scale):
    rows, cols = depth.shape
    half = 0.5 * scale
    east = half * (depth + roll(depth, -1, 1))
    north = half * (depth + roll(depth, -1, 0))
    east = jnp.where(index_of(depth.shape, 1) < cols - 1, east, 0.0)
    north = jnp.where(index_of(depth.shape, 0) < rows - 1, north, 0.0)
    return east, north


def fine_step(s, e, n, face_x, face_y):
    slope_x = [roll(v, -1, 1) - v for v in s]
    slope_y = [s[1] - s[0], roll(s[0], -1, 0) - s[1]]
    e = [v + f * d for v, f, d in zip(e, face_x, slope_x)]
    n = [v + f * d for v, f, d in zip(n, face_y, slope_y)]
    flow_y = [n[0] - roll(n[1], 1, 0), n[1] - n[0]]
    s = [v + ((x - roll(x, 1, 1)) + y) for v, x, y in zip(s, e, flow_y)]
    return s, e, n, slope_x, slope_y


def inside_x(pair):
    cols = pair[0].shape[1]
    keep = index_of(pair[0].shape, 1) < cols - 1
    return [jnp.where(keep, v, 0.0) for v in pair]


def inside_y(pair):
    rows = pair[1].shape[0]
    return [pair[0], jnp.where(index_of(pair[1].shape, 0) < rows - 1, pair[1], 0.0)]


def rows_of(ref, *at):
    half = ref.shape[-2] // 2
    return [
        jnp.concatenate(
            [ref[(v, *at, pl.ds(parity, half, stride=2), slice(None))] for v in range(ref.shape[0])], axis=1
        )
        for parity in range(2)
    ]


def spread_copies(source, stage, sem):
    lead = (slice(None),) * (len(source.shape) - 1)
    return [
        pltpu.make_async_copy(source.at[(*lead, pl.ds(v * LANES, LANES))], stage.at[v], sem)
        for v in range(stage.shape[0])
    ]


def wait_all(stage, sem):
    pltpu.make_async_copy(stage, stage, sem).wait()


def thirds(value):
    high = value.astype(jnp.bfloat16)
    rest = value - high.astype(jnp.float32)
    mid = rest.astype(jnp.bfloat16)
    low = (rest - mid.astype(jnp.float32)).astype(jnp.bfloat16)
    return jnp.concatenate([high, mid, low], axis=1)


def stacked(fields):
    rows = sum(field.shape[0] for field in fields)
    pad = -rows % 16
    if pad:
        fields = list(fields) + [jnp.zeros((pad, fields[0].shape[1]), jnp.float32)]
    return jnp.concatenate(fields, axis=0)


def restrict_pairs(pairs):
    half, cols = pairs[0][0].shape
    sums = stacked([even + odd for even, odd in pairs])
    gather = pair_matrix((2 * LANES, LANES), 0, 0.25).astype(jnp.bfloat16)
    gather = jnp.concatenate([gather] * 3, axis=0)
    merged = jnp.concatenate(
        [
            jnp.dot(thirds(sums[:, c : c + 2 * LANES]), gather, preferred_element_type=jnp.float32)
            for c in range(0, cols, 2 * LANES)
        ],
        axis=1,
    )
    return [merged[i * half : (i + 1) * half] for i in range(len(pairs))]


def prolong_columns(fields):
    half, cols = fields[0].shape
    rows = stacked(fields)
    spread = pair_matrix((LANES, 2 * LANES), 1, 1.0).astype(jnp.bfloat16)
    spread = jnp.concatenate([spread] * 3, axis=0)
    merged = jnp.concatenate(
        [
            jnp.dot(thirds(rows[:, c : c + LANES]), spread, preferred_element_type=jnp.float32)
            for c in range(0, cols, LANES)
        ],
        axis=1,
    )
    return [merged[i * half : (i + 1) * half] for i in range(len(fields))]


def coarse_step(fields, face_x, face_y):
    return power(fields, 1, face_x, face_y)


def power(fields, count, face_x, face_y):
    if count == 0:
        return fields
    s, e, n = fields
    rows, cols = s.shape
    inner_x = index_of(s.shape, 1) < cols - 1
    inner_y = index_of(s.shape, 0) < rows - 1
    e_in, n_in = jnp.where(inner_x, e, 0.0), jnp.where(inner_y, n, 0.0)
    e_edge, n_edge = e - e_in, n - n_in
    face_x = jnp.where(inner_x, face_x, 0.0)

    def body(_, carried):
        s, e, n = carried
        e = e + face_x * (roll(s, -1, 1) - s)
        n = n + face_y * (roll(s, -1, 0) - s)
        return s + ((e - roll(e, 1, 1)) + (n - roll(n, 1, 0))), e, n

    carried = (s, e_in, n_in)
    if count <= 4:
        for step in range(count):
            carried = body(step, carried)
    else:
        carried = lax.fori_loop(0, count, body, carried)
    s, e, n = carried
    return s, e + e_edge, n + n_edge


def add(a, b):
    return tuple(x + y for x, y in zip(a, b))


def scaled(a, factor):
    return tuple(x * factor for x in a)


def pick(first, a, b):
    return tuple(jnp.where(first, x, y) for x, y in zip(a, b))


def read(ref, at=0):
    return tuple(ref[at + i] for i in range(3))


def write(ref, fields, at=0):
    for i, field in enumerate(fields):
        ref[at + i] = field


def pair_matrix(shape, wide_axis, weight):
    wide = index_of(shape, wide_axis) // 2
    return jnp.where(wide == index_of(shape, 1 - wide_axis), weight, 0.0)


def product(a, b):
    return jnp.dot(a, b, precision=EXACT, preferred_element_type=jnp.float32)


def prolong_all(fields):
    half, cols = fields[0].shape
    stacked = jnp.concatenate(fields, axis=0)
    stacked = product(pair_matrix((2 * stacked.shape[0], stacked.shape[0]), 0, 1.0), stacked)
    spread = pair_matrix((LANES, 2 * LANES), 1, 1.0)
    merged = jnp.concatenate(
        [product(stacked[:, c : c + LANES], spread) for c in range(0, cols, LANES)], axis=1
    )
    return [merged[2 * i * half : 2 * (i + 1) * half] for i in range(len(fields))]


def prepare(
    table_in,
    levels,
    wet,
    initial,
    forcing,
    own,
    sent,
    planes,
    coarse_faces,
    table,
    stage_l,
    stage_w,
    stage_i,
    stage_f,
    sems,
):
    load_table = pltpu.make_async_copy(table_in, table, sems.at[4])
    load_table.start()
    sources = ((levels, stage_l), (wet, stage_w), (initial.at[0], stage_i), (forcing, stage_f))
    for i, (source, stage) in enumerate(sources):
        for copy in spread_copies(source, stage, sems.at[i]):
            copy.start()
    steps = forcing.shape[0]
    width = own.shape[2]
    coarse_cols = levels.shape[1] // 2
    load_table.wait()
    wait_all(stage_l, sems.at[0])
    level = rows_of(stage_l)
    depth = [jnp.zeros(v.shape, jnp.float32) for v in level]
    for i in range(table.shape[0]):
        depth = [jnp.where(v == i, table[i], d) for v, d in zip(level, depth)]
    wait_all(stage_w, sems.at[1])
    dry = [v.astype(jnp.float32) for v in rows_of(stage_w)]
    depth = [d * v for d, v in zip(depth, dry)]
    half = 0.5 * COURANT * COURANT
    face_x = inside_x([half * (d + roll(d, -1, 1)) for d in depth])
    face_y = inside_y([half * (depth[0] + depth[1]), half * (depth[1] + roll(depth[0], -1, 0))])
    for i, plane in enumerate(face_x + face_y + dry):
        planes[i] = plane

    wait_all(stage_i, sems.at[2])
    s0 = rows_of(stage_i, 0)
    e0 = [v * COURANT for v in rows_of(stage_i, 1)]
    n0 = [v * COURANT for v in rows_of(stage_i, 2)]
    e_in, n_in = inside_x(e0), inside_y(n0)
    s, e, n = s0, e_in, n_in
    for _ in range(steps):
        s, e, n, _, _ = fine_step(s, e, n, face_x, face_y)
    e = [v + (x - y) for v, x, y in zip(e, e0, e_in)]
    n = [v + (x - y) for v, x, y in zip(n, n0, n_in)]
    relaxed = [s, e, n]

    wait_all(stage_f, sems.at[3])
    s = rows_of(stage_f, steps - 1)
    e = [jnp.zeros_like(v) for v in s]
    n = e
    for step in reversed(range(steps - 1)):
        s, e, n, _, _ = fine_step(s, e, n, face_x, face_y)
        s = [v + f for v, f in zip(s, rows_of(stage_f, step))]
    for pair, start in zip((s, e, n), (s0, e0, n0)):
        relaxed.append([v - x for v, x in zip(pair, start)])
    su, eu, nu, sw, ew, nw, coarse_depth = restrict_pairs(relaxed + [depth])
    ratio = steps / 2
    coarse_courant = COURANT * ratio
    cx, cy = faces(coarse_depth, coarse_courant * coarse_courant)
    w = (sw, ew * ratio, nw * ratio)
    g = add((su, eu * ratio, nu * ratio), coarse_step(w, cx, cy))

    core = lax.rem(lax.axis_index("tm"), 2)
    right = coarse_cols - width

    def store(mine, other):
        for ref, at in ((own, mine), (sent, other)):
            for i in range(3):
                ref[i] = g[i][:, at : at + width]
                ref[3 + i] = w[i][:, at : at + width]
        coarse_faces[0] = cx[:, mine : mine + width]
        coarse_faces[1] = cy[:, mine : mine + width]

    @pl.when(core == 0)
    def _():
        store(0, right)

    @pl.when(core == 1)
    def _():
        store(right, 0)


def chip_pair(own, got, coarse_faces, out):
    cx, cy = coarse_faces[0], coarse_faces[1]
    first = lax.rem(lax.axis_index("tm"), 2) == 0
    g_own, g_got = read(own), read(got)
    g_low, g_high = pick(first, g_own, g_got), pick(first, g_got, g_own)
    w_low = pick(first, read(own, 3), read(got, 3))
    write(out, add(g_low, coarse_step(g_high, cx, cy)))
    write(out, add(w_low, g_high), 3)


def row_pair(own, got, coarse_faces, out, out_t):
    cx, cy = coarse_faces[0], coarse_faces[1]
    first = lax.rem(lax.axis_index("tm") // 2, 2) == 0
    t_own, t_got = read(own), read(got)
    t_low, t_high = pick(first, t_own, t_got), pick(first, t_got, t_own)
    q_low = pick(first, read(own, 3), read(got, 3))
    moved = coarse_step(t_high, cx, cy)
    total = add(t_low, coarse_step(moved, cx, cy))
    write(out, total)
    write(out_t, total)
    write(out, add(q_low, moved), 3)


def widen(stride, own, got, coarse_faces, out, *, per_row, rows_in_all):
    row = lax.axis_index("tm") // per_row
    there = jnp.where(row + stride < rows_in_all, 1.0, 0.0)
    moved = power(scaled(read(got), there), per_row * stride, coarse_faces[0], coarse_faces[1])
    write(out, add(read(own), moved))


def finish(near, far, farther, own, got, chip, partner, coarse_faces, kept, sent, *, per_row, rows_in_all):
    cx, cy = coarse_faces[0], coarse_faces[1]
    width = coarse_faces.shape[2]
    half = kept.shape[2]
    device = lax.axis_index("tm")
    row = device // per_row

    def there(stride):
        return jnp.where(row + stride < rows_in_all, 1.0, 0.0)

    rest = scaled(read(far), there(2))
    if farther is not None:
        rest = add(rest, power(scaled(read(farther), there(3)), per_row, cx, cy))
    rest = power(rest, per_row - 1, cx, cy)
    after = add(scaled(read(near, 3), there(1)), rest)
    end = add(scaled(read(near), there(1)), coarse_step(rest, cx, cy))
    if partner is not None:
        low = lax.rem(device // 2, 2) == 0
        moved = coarse_step(end, cx, cy)
        after = pick(low, add(read(partner, 3), moved), after)
        end = pick(low, add(read(partner), coarse_step(moved, cx, cy)), end)
    first = lax.rem(device, 2) == 0
    w_high = pick(first, read(got, 3), read(own, 3))
    q = read(chip, 3)
    c_low = add(q, coarse_step(end, cx, cy))
    c_high = add(w_high, end)

    @pl.when(first)
    def _():
        for i in range(3):
            kept[i] = c_low[i][:, :half]
            kept[3 + i] = c_high[i][:, :half]
            sent[i] = c_high[i][:, :half]
            sent[3 + i] = after[i][:, :half]

    @pl.when(jnp.logical_not(first))
    def _():
        for i in range(3):
            kept[i] = c_high[i][:, width - half :]
            kept[3 + i] = after[i][:, width - half :]
            sent[i] = c_low[i][:, width - half :]
            sent[3 + i] = c_high[i][:, width - half :]


def joined(kept, got, at):
    first = lax.rem(lax.axis_index("tm"), 2) == 0
    fields = []
    for i in range(at, at + 3):
        left = jnp.where(first, kept[i], got[i])
        right = jnp.where(first, got[i], kept[i])
        fields.append(jnp.concatenate([left, right], axis=1))
    return fields


def correct(kept, got, initial_in, corrected, done, initial, sem, *, steps):
    load = pltpu.make_async_copy(initial_in, initial, sem)
    load.start()
    done[...] = jnp.zeros_like(done)
    unscale = 1.0 / (COURANT * (steps / 2))
    s, e, n = joined(kept, got, 0)
    fields = prolong_all([s, e * unscale, n * unscale])
    load.wait()
    for i, field in enumerate(fields):
        corrected[0, i] = initial[0, i] + field


def pulled(slopes, dry):
    grad_x, grad_y = inside_x(slopes[0]), inside_y(slopes[1])
    across = [grad_y[0] + roll(grad_y[1], 1, 0), grad_y[1] + grad_y[0]]
    return [
        (0.5 * COURANT) * ((x + roll(x, 1, 1)) + y) * keep for x, y, keep in zip(grad_x, across, dry)
    ]


def base(order, following, forcing, velocity, planes, flow, grad, stage_i, stage_f, sems):
    sources = ((following.at[0], stage_i), (forcing, stage_f), (velocity, flow))
    for i, (source, stage) in enumerate(sources):
        for copy in spread_copies(source, stage, sems.at[i]):
            copy.start()
    steps = forcing.shape[0]
    device = lax.axis_index("tm")
    there = jnp.where(device + 1 < lax.axis_size("tm"), 1.0, 0.0)
    face_x, face_y = [planes[0], planes[1]], [planes[2], planes[3]]
    wait_all(stage_i, sems.at[0])
    s = [v * there for v in rows_of(stage_i, 0)]
    e = inside_x([v * (there * COURANT) for v in rows_of(stage_i, 1)])
    n = inside_y([v * (there * COURANT) for v in rows_of(stage_i, 2)])
    wait_all(stage_f, sems.at[1])
    wait_all(flow, sems.at[2])
    sums = [[jnp.zeros_like(v) for v in s] for _ in range(2)]
    for step in reversed(range(steps)):
        s, e, n, *slopes = fine_step(s, e, n, face_x, face_y)
        for k in range(2):
            sums[k] = [a + d * v for a, d, v in zip(sums[k], slopes[k], rows_of(flow, step, k))]
        if step:
            s = [v + f for v, f in zip(s, rows_of(stage_f, step))]
    for i, value in enumerate(pulled(sums, [planes[4], planes[5]])):
        grad[i] = value


def descend(kept, got, flow, planes, grad, mine, other):
    steps = flow.shape[1]
    half = mine.shape[2]
    first = lax.rem(lax.axis_index("tm"), 2) == 0
    inverse = 1.0 / (steps / 2)
    s, e, n = prolong_columns(joined(kept, got, 3))
    e, n = e * inverse, n * inverse
    s, e, n = [s, s], inside_x([e, e]), inside_y([n, n])
    face_x, face_y = [planes[0], planes[1]], [planes[2], planes[3]]
    sums = [[jnp.zeros_like(v) for v in s] for _ in range(2)]
    for step in reversed(range(steps)):
        s, e, n, *slopes = fine_step(s, e, n, face_x, face_y)
        for k in range(2):
            sums[k] = [a + d * v for a, d, v in zip(sums[k], slopes[k], rows_of(flow, step, k))]
    total = [grad[i] + v for i, v in enumerate(pulled(sums, [planes[4], planes[5]]))]

    @pl.when(first)
    def _():
        for i in range(2):
            mine[i] = total[i][:, :half]
            other[i] = total[i][:, half:]

    @pl.when(jnp.logical_not(first))
    def _():
        for i in range(2):
            mine[i] = total[i][:, half:]
            other[i] = total[i][:, :half]


def plus(a, b, order, out):
    out[...] = a[...] + b[...]


def weave(mine, other, out, stage, sem):
    first = lax.rem(lax.axis_index("tm"), 2) == 0
    half = stage.shape[1] // 2
    blocks = stage.shape[0] // 2
    for i in range(2):
        left, right = jnp.where(first, mine[i], other[i]), jnp.where(first, other[i], mine[i])
        for v in range(blocks):
            at = slice(v * LANES, (v + 1) * LANES)
            stage[v, pl.ds(i, half, stride=2), :] = left[:, at]
            stage[blocks + v, pl.ds(i, half, stride=2), :] = right[:, at]
    for v in range(2 * blocks):
        pltpu.make_async_copy(stage.at[v], out.at[:, pl.ds(v * LANES, LANES)], sem).start()
    wait_all(stage, sem)


def call(body, shapes, operands, *, specs=None, outs=None, scratch=(), cost=1000):
    return pl.pallas_call(
        body,
        out_shape=[jax.ShapeDtypeStruct(shape, jnp.float32) for shape in shapes],
        in_specs=specs or [VMEM] * len(operands),
        out_specs=outs or [VMEM] * len(shapes),
        scratch_shapes=scratch,
        cost_estimate=pl.CostEstimate(flops=cost, bytes_accessed=cost, transcendentals=0),
        compiler_params=pltpu.CompilerParams(vmem_limit_bytes=32 * 1024 * 1024),
    )(*operands)


def shards(initial, velocity, forcing, depth_table, levels, wet_mask):
    count = lax.axis_size("tm")
    rows, cols = levels.shape
    steps = forcing.shape[0]
    half_rows, half = rows // 2, cols // 4
    halo = -(-count // LANES) * LANES
    width = half + halo
    block = (half_rows, width)
    blocks = cols // LANES
    plane = (half_rows, cols)

    def paired(value, stride):
        return lax.ppermute(value, "tm", [(s, s ^ stride) for s in range(count)])

    def back(value, stride):
        return lax.ppermute(value, "tm", [(s, (s - stride) % count) for s in range(count)])

    def stage(*lead, kind=jnp.float32):
        return pltpu.VMEM((blocks, *lead, rows, LANES), kind)

    initial, velocity, forcing, depth_table, levels, wet_mask = (
        pltpu.with_memory_space_constraint(value, pltpu.HBM)
        for value in (initial, velocity, forcing, depth_table, levels, wet_mask)
    )
    following = lax.ppermute(initial, "tm", [(s, s - 1) for s in range(1, count)])
    own, sent, planes, coarse_faces = call(
        prepare,
        [(6, *block), (6, *block), (6, *plane), (2, *block)],
        [depth_table, levels, wet_mask, initial, forcing],
        specs=[HBM] * 5,
        scratch=[
            pltpu.SMEM(depth_table.shape, jnp.float32),
            stage(kind=jnp.int32),
            stage(kind=jnp.int32),
            stage(3),
            stage(steps),
            pltpu.SemaphoreType.DMA((5,)),
        ],
        cost=PREPARE_COST,
    )
    got = paired(sent, 1)
    (chip,) = call(chip_pair, [(6, *block)], [own, got, coarse_faces])
    per_row = 4 if count <= 16 else 2
    rows_in_all = count // per_row
    if per_row == 4:
        partner = paired(chip, 2)
        row, row_t = call(row_pair, [(6, *block), (3, *block)], [chip, partner, coarse_faces])
    else:
        partner = None
        row, row_t = chip, chip[:3]
    near = back(row, per_row)
    if rows_in_all <= 4:
        far, farther = back(row_t, 2 * per_row), back(row_t, 3 * per_row)
    else:
        stride = 1
        while stride < rows_in_all - 2:
            (row_t,) = call(
                functools.partial(widen, stride, per_row=per_row, rows_in_all=rows_in_all),
                [(3, *block)],
                [row_t, back(row_t, stride * per_row), coarse_faces],
            )
            stride *= 2
        far, farther = back(row_t, 2 * per_row), None

    flow, grad = call(
        base,
        [(blocks, steps, 2, rows, LANES), (2, *plane)],
        [row_t, following, forcing, velocity, planes],
        specs=[ANY, ANY, HBM, HBM, VMEM],
        scratch=[stage(3), stage(steps), pltpu.SemaphoreType.DMA((3,))],
        cost=BASE_COST,
    )

    operands = {
        "near": near,
        "far": far,
        "farther": farther,
        "own": own,
        "got": got,
        "chip": chip,
        "partner": partner,
        "coarse_faces": coarse_faces,
    }
    names = [name for name, value in operands.items() if value is not None]

    def finish_body(*refs):
        given = dict.fromkeys(operands)
        given.update(zip(names, refs))
        kept, sent = refs[len(names) + 1 :]
        finish(**given, kept=kept, sent=sent, per_row=per_row, rows_in_all=rows_in_all)

    kept, sent = call(
        finish_body,
        [(6, half_rows, half)] * 2,
        [operands[name] for name in names] + [grad],
        specs=[VMEM] * len(names) + [ANY],
    )
    got = paired(sent, 1)
    mine, other = call(
        descend, [(2, half_rows, cols // 2)] * 2, [kept, got, flow, planes, grad], cost=BASE_COST
    )
    mine = mine + paired(other, 1)
    corrected, done = call(
        functools.partial(correct, steps=steps),
        [initial.shape, (8, LANES)],
        [kept, got, initial],
        specs=[VMEM, VMEM, HBM],
        scratch=[pltpu.VMEM(initial.shape, jnp.float32), pltpu.SemaphoreType.DMA],
        cost=CORRECT_COST,
    )
    if per_row == 4:
        (mine,) = call(plus, [mine.shape], [mine, paired(mine, 2), done], specs=[VMEM, VMEM, ANY])
    if rows_in_all == 4:
        mine = mine + paired(mine, 4) + paired(mine, 8) + paired(mine, 12)
    else:
        stride = per_row
        while stride < count:
            mine = mine + paired(mine, stride)
            stride *= 2
    (gradient,) = call(
        weave,
        [(rows, cols)],
        [mine, paired(mine, 1)],
        outs=[HBM],
        scratch=[stage(), pltpu.SemaphoreType.DMA],
    )
    return corrected, gradient


def solution(mesh):
    in_specs = (
        P("tm", "parts", None, None),
        P("tm", "parts", None, None),
        P("tm", "parts", None),
        P(),
        P("parts", None),
        P("parts", None),
    )
    out_specs = (P("tm", "parts", None, None), P("parts", None))
    return jax.shard_map(shards, mesh=mesh, in_specs=in_specs, out_specs=out_specs, check_vma=False)
```

```python
import functools

import jax
import jax.numpy as jnp
from jax import lax
from jax.experimental import pallas as pl
from jax.experimental.pallas import tpu as pltpu
from jax.sharding import PartitionSpec as P

COURANT = 0.06
LANES = 128
SUBLANES = 8
VMEM = pl.BlockSpec(memory_space=pltpu.VMEM)
HBM = pl.BlockSpec(memory_space=pltpu.HBM)
ANY = pl.BlockSpec(memory_space=pl.ANY)
PREPARE_COST = 40_000_000
BASE_COST = 8_000_000
CORRECT_COST = 4_000_000
EXACT = lax.Precision.HIGHEST


def roll(value, steps, axis):
    return pltpu.roll(value, steps % value.shape[axis], axis)


def index_of(shape, axis):
    return lax.broadcasted_iota(jnp.int32, shape, axis)


def faces(depth, scale):
    rows, cols = depth.shape
    half = 0.5 * scale
    east = half * (depth + roll(depth, -1, 1))
    north = half * (depth + roll(depth, -1, 0))
    east = jnp.where(index_of(depth.shape, 1) < cols - 1, east, 0.0)
    north = jnp.where(index_of(depth.shape, 0) < rows - 1, north, 0.0)
    return east, north


def fine_step(s, e, n, face_x, face_y):
    slope_x = [roll(v, -1, 1) - v for v in s]
    slope_y = [s[1] - s[0], roll(s[0], -1, 0) - s[1]]
    e = [v + f * d for v, f, d in zip(e, face_x, slope_x)]
    n = [v + f * d for v, f, d in zip(n, face_y, slope_y)]
    flow_y = [n[0] - roll(n[1], 1, 0), n[1] - n[0]]
    s = [v + ((x - roll(x, 1, 1)) + y) for v, x, y in zip(s, e, flow_y)]
    return s, e, n, slope_x, slope_y


def inside_x(pair):
    cols = pair[0].shape[1]
    keep = index_of(pair[0].shape, 1) < cols - 1
    return [jnp.where(keep, v, 0.0) for v in pair]


def inside_y(pair):
    rows = pair[1].shape[0]
    return [pair[0], jnp.where(index_of(pair[1].shape, 0) < rows - 1, pair[1], 0.0)]


def rows_of(ref, *at):
    half = ref.shape[-2] // 2
    return [
        jnp.concatenate(
            [ref[(*at, v, pl.ds(parity, half, stride=2), slice(None))] for v in range(ref.shape[-3])], axis=1
        )
        for parity in range(2)
    ]


def spread_copies(source, stage, sem):
    lead = (slice(None),) * (len(source.shape) - 4)
    return [
        pltpu.make_async_copy(
            source.at[(*lead, tile)], stage.at[(*lead, slice(None), pl.ds(tile * SUBLANES, SUBLANES))], sem
        )
        for tile in range(source.shape[-4])
    ]


def tiled(value):
    *lead, rows, cols = value.shape
    value = value.reshape(*lead, rows // SUBLANES, SUBLANES, cols // LANES, LANES)
    return jnp.swapaxes(value, -2, -3)


def wait_all(stage, sem):
    pltpu.make_async_copy(stage, stage, sem).wait()


def thirds(value):
    high = value.astype(jnp.bfloat16)
    rest = value - high.astype(jnp.float32)
    mid = rest.astype(jnp.bfloat16)
    low = (rest - mid.astype(jnp.float32)).astype(jnp.bfloat16)
    return jnp.concatenate([high, mid, low], axis=1)


def stacked(fields):
    rows = sum(field.shape[0] for field in fields)
    pad = -rows % 16
    if pad:
        fields = list(fields) + [jnp.zeros((pad, fields[0].shape[1]), jnp.float32)]
    return jnp.concatenate(fields, axis=0)


def restrict_pairs(pairs):
    half, cols = pairs[0][0].shape
    sums = stacked([even + odd for even, odd in pairs])
    gather = pair_matrix((2 * LANES, LANES), 0, 0.25).astype(jnp.bfloat16)
    gather = jnp.concatenate([gather] * 3, axis=0)
    merged = jnp.concatenate(
        [
            jnp.dot(thirds(sums[:, c : c + 2 * LANES]), gather, preferred_element_type=jnp.float32)
            for c in range(0, cols, 2 * LANES)
        ],
        axis=1,
    )
    return [merged[i * half : (i + 1) * half] for i in range(len(pairs))]


def prolong_columns(fields):
    half, cols = fields[0].shape
    rows = stacked(fields)
    spread = pair_matrix((LANES, 2 * LANES), 1, 1.0).astype(jnp.bfloat16)
    spread = jnp.concatenate([spread] * 3, axis=0)
    merged = jnp.concatenate(
        [
            jnp.dot(thirds(rows[:, c : c + LANES]), spread, preferred_element_type=jnp.float32)
            for c in range(0, cols, LANES)
        ],
        axis=1,
    )
    return [merged[i * half : (i + 1) * half] for i in range(len(fields))]


def coarse_step(fields, face_x, face_y):
    return power(fields, 1, face_x, face_y)


def power(fields, count, face_x, face_y):
    if count == 0:
        return fields
    s, e, n = fields
    rows, cols = s.shape
    inner_x = index_of(s.shape, 1) < cols - 1
    inner_y = index_of(s.shape, 0) < rows - 1
    e_in, n_in = jnp.where(inner_x, e, 0.0), jnp.where(inner_y, n, 0.0)
    e_edge, n_edge = e - e_in, n - n_in
    face_x = jnp.where(inner_x, face_x, 0.0)
    face_w, face_s = roll(face_x, 1, 1), roll(face_y, 1, 0)

    def body(_, carried):
        s, e, n, west, south = carried
        e = e + face_x * (roll(s, -1, 1) - s)
        n = n + face_y * (roll(s, -1, 0) - s)
        west = west + face_w * (s - roll(s, 1, 1))
        south = south + face_s * (s - roll(s, 1, 0))
        return s + ((e - west) + (n - south)), e, n, west, south

    carried = (s, e_in, n_in, roll(e_in, 1, 1), roll(n_in, 1, 0))
    if count <= 4:
        for step in range(count):
            carried = body(step, carried)
    else:
        carried = lax.fori_loop(0, count, body, carried)
    s, e, n, _, _ = carried
    return s, e + e_edge, n + n_edge


def add(a, b):
    return tuple(x + y for x, y in zip(a, b))


def scaled(a, factor):
    return tuple(x * factor for x in a)


def pick(first, a, b):
    return tuple(jnp.where(first, x, y) for x, y in zip(a, b))


def read(ref, at=0):
    return tuple(ref[at + i] for i in range(3))


def write(ref, fields, at=0):
    for i, field in enumerate(fields):
        ref[at + i] = field


def pair_matrix(shape, wide_axis, weight):
    wide = index_of(shape, wide_axis) // 2
    return jnp.where(wide == index_of(shape, 1 - wide_axis), weight, 0.0)


def product(a, b):
    return jnp.dot(a, b, precision=EXACT, preferred_element_type=jnp.float32)


def prolong_all(fields):
    half, cols = fields[0].shape
    stacked = jnp.concatenate(fields, axis=0)
    stacked = product(pair_matrix((2 * stacked.shape[0], stacked.shape[0]), 0, 1.0), stacked)
    spread = pair_matrix((LANES, 2 * LANES), 1, 1.0)
    merged = jnp.concatenate(
        [product(stacked[:, c : c + LANES], spread) for c in range(0, cols, LANES)], axis=1
    )
    return [merged[2 * i * half : 2 * (i + 1) * half] for i in range(len(fields))]


def prepare(
    table_in,
    levels,
    wet,
    initial,
    forcing,
    own,
    sent,
    planes,
    coarse_faces,
    table,
    stage_l,
    stage_w,
    stage_i,
    stage_f,
    sems,
):
    load_table = pltpu.make_async_copy(table_in, table, sems.at[4])
    load_table.start()
    sources = ((levels, stage_l), (wet, stage_w), (initial.at[0], stage_i), (forcing, stage_f))
    for i, (source, stage) in enumerate(sources):
        for copy in spread_copies(source, stage, sems.at[i]):
            copy.start()
    steps = forcing.shape[0]
    width = own.shape[2]
    coarse_cols = stage_l.shape[0] * LANES // 2
    load_table.wait()
    wait_all(stage_l, sems.at[0])
    level = rows_of(stage_l)
    depth = [jnp.zeros(v.shape, jnp.float32) for v in level]
    for i in range(table.shape[0]):
        depth = [jnp.where(v == i, table[i], d) for v, d in zip(level, depth)]
    wait_all(stage_w, sems.at[1])
    dry = [v.astype(jnp.float32) for v in rows_of(stage_w)]
    depth = [d * v for d, v in zip(depth, dry)]
    half = 0.5 * COURANT * COURANT
    face_x = inside_x([half * (d + roll(d, -1, 1)) for d in depth])
    face_y = inside_y([half * (depth[0] + depth[1]), half * (depth[1] + roll(depth[0], -1, 0))])
    for i, plane in enumerate(face_x + face_y + dry):
        planes[i] = plane

    wait_all(stage_i, sems.at[2])
    s0 = rows_of(stage_i, 0)
    e0 = [v * COURANT for v in rows_of(stage_i, 1)]
    n0 = [v * COURANT for v in rows_of(stage_i, 2)]
    e_in, n_in = inside_x(e0), inside_y(n0)
    s, e, n = s0, e_in, n_in
    for _ in range(steps):
        s, e, n, _, _ = fine_step(s, e, n, face_x, face_y)
    e = [v + (x - y) for v, x, y in zip(e, e0, e_in)]
    n = [v + (x - y) for v, x, y in zip(n, n0, n_in)]
    relaxed = [s, e, n]

    wait_all(stage_f, sems.at[3])
    s = rows_of(stage_f, steps - 1)
    e = [jnp.zeros_like(v) for v in s]
    n = e
    for step in reversed(range(steps - 1)):
        s, e, n, _, _ = fine_step(s, e, n, face_x, face_y)
        s = [v + f for v, f in zip(s, rows_of(stage_f, step))]
    for pair, start in zip((s, e, n), (s0, e0, n0)):
        relaxed.append([v - x for v, x in zip(pair, start)])
    su, eu, nu, sw, ew, nw, coarse_depth = restrict_pairs(relaxed + [depth])
    ratio = steps / 2
    coarse_courant = COURANT * ratio
    cx, cy = faces(coarse_depth, coarse_courant * coarse_courant)
    w = (sw, ew * ratio, nw * ratio)
    g = add((su, eu * ratio, nu * ratio), coarse_step(w, cx, cy))

    core = lax.rem(lax.axis_index("tm"), 2)
    right = coarse_cols - width

    def store(mine, other):
        for ref, at in ((own, mine), (sent, other)):
            for i in range(3):
                ref[i] = g[i][:, at : at + width]
                ref[3 + i] = w[i][:, at : at + width]
        coarse_faces[0] = cx[:, mine : mine + width]
        coarse_faces[1] = cy[:, mine : mine + width]

    @pl.when(core == 0)
    def _():
        store(0, right)

    @pl.when(core == 1)
    def _():
        store(right, 0)


def chip_pair(own, got, coarse_faces, out):
    cx, cy = coarse_faces[0], coarse_faces[1]
    first = lax.rem(lax.axis_index("tm"), 2) == 0
    g_own, g_got = read(own), read(got)
    g_low, g_high = pick(first, g_own, g_got), pick(first, g_got, g_own)
    w_low = pick(first, read(own, 3), read(got, 3))
    write(out, add(g_low, coarse_step(g_high, cx, cy)))
    write(out, add(w_low, g_high), 3)


def row_pair(own, got, coarse_faces, out, out_t):
    cx, cy = coarse_faces[0], coarse_faces[1]
    first = lax.rem(lax.axis_index("tm") // 2, 2) == 0
    t_own, t_got = read(own), read(got)
    t_low, t_high = pick(first, t_own, t_got), pick(first, t_got, t_own)
    q_low = pick(first, read(own, 3), read(got, 3))
    moved = coarse_step(t_high, cx, cy)
    total = add(t_low, coarse_step(moved, cx, cy))
    write(out, total)
    write(out_t, total)
    write(out, add(q_low, moved), 3)


def widen(stride, own, got, coarse_faces, out, *, per_row, rows_in_all):
    row = lax.axis_index("tm") // per_row
    there = jnp.where(row + stride < rows_in_all, 1.0, 0.0)
    moved = power(scaled(read(got), there), per_row * stride, coarse_faces[0], coarse_faces[1])
    write(out, add(read(own), moved))


def finish(near, far, farther, own, got, chip, partner, coarse_faces, kept, sent, *, per_row, rows_in_all):
    cx, cy = coarse_faces[0], coarse_faces[1]
    width = coarse_faces.shape[2]
    half = kept.shape[2]
    device = lax.axis_index("tm")
    row = device // per_row

    def there(stride):
        return jnp.where(row + stride < rows_in_all, 1.0, 0.0)

    rest = scaled(read(far), there(2))
    if farther is not None:
        rest = add(rest, power(scaled(read(farther), there(3)), per_row, cx, cy))
    rest = power(rest, per_row - 1, cx, cy)
    after = add(scaled(read(near, 3), there(1)), rest)
    end = add(scaled(read(near), there(1)), coarse_step(rest, cx, cy))
    if partner is not None:
        low = lax.rem(device // 2, 2) == 0
        moved = coarse_step(end, cx, cy)
        after = pick(low, add(read(partner, 3), moved), after)
        end = pick(low, add(read(partner), coarse_step(moved, cx, cy)), end)
    first = lax.rem(device, 2) == 0
    w_high = pick(first, read(got, 3), read(own, 3))
    q = read(chip, 3)
    c_low = add(q, coarse_step(end, cx, cy))
    c_high = add(w_high, end)

    @pl.when(first)
    def _():
        for i in range(3):
            kept[i] = c_low[i][:, :half]
            kept[3 + i] = c_high[i][:, :half]
            sent[i] = c_high[i][:, :half]
            sent[3 + i] = after[i][:, :half]

    @pl.when(jnp.logical_not(first))
    def _():
        for i in range(3):
            kept[i] = c_high[i][:, width - half :]
            kept[3 + i] = after[i][:, width - half :]
            sent[i] = c_low[i][:, width - half :]
            sent[3 + i] = c_high[i][:, width - half :]


def joined(kept, got, at):
    first = lax.rem(lax.axis_index("tm"), 2) == 0
    fields = []
    for i in range(at, at + 3):
        left = jnp.where(first, kept[i], got[i])
        right = jnp.where(first, got[i], kept[i])
        fields.append(jnp.concatenate([left, right], axis=1))
    return fields


def correct(kept, got, initial_in, corrected, done, initial, sem, *, steps):
    load = pltpu.make_async_copy(initial_in, initial, sem)
    load.start()
    done[...] = jnp.zeros_like(done)
    unscale = 1.0 / (COURANT * (steps / 2))
    s, e, n = joined(kept, got, 0)
    fields = prolong_all([s, e * unscale, n * unscale])
    load.wait()
    for i, field in enumerate(fields):
        corrected[0, i] = initial[0, i] + field


def pulled(slopes, dry):
    grad_x, grad_y = inside_x(slopes[0]), inside_y(slopes[1])
    across = [grad_y[0] + roll(grad_y[1], 1, 0), grad_y[1] + grad_y[0]]
    return [
        (0.5 * COURANT) * ((x + roll(x, 1, 1)) + y) * keep for x, y, keep in zip(grad_x, across, dry)
    ]


def base(order, following, forcing, velocity, planes, flow, grad, stage_i, stage_f, sems):
    sources = ((following.at[0], stage_i), (forcing, stage_f), (velocity, flow))
    for i, (source, stage) in enumerate(sources):
        for copy in spread_copies(source, stage, sems.at[i]):
            copy.start()
    steps = forcing.shape[0]
    device = lax.axis_index("tm")
    there = jnp.where(device + 1 < lax.axis_size("tm"), 1.0, 0.0)
    face_x, face_y = [planes[0], planes[1]], [planes[2], planes[3]]
    wait_all(stage_i, sems.at[0])
    s = [v * there for v in rows_of(stage_i, 0)]
    e = inside_x([v * (there * COURANT) for v in rows_of(stage_i, 1)])
    n = inside_y([v * (there * COURANT) for v in rows_of(stage_i, 2)])
    wait_all(stage_f, sems.at[1])
    wait_all(flow, sems.at[2])
    sums = [[jnp.zeros_like(v) for v in s] for _ in range(2)]
    for step in reversed(range(steps)):
        s, e, n, *slopes = fine_step(s, e, n, face_x, face_y)
        for k in range(2):
            sums[k] = [a + d * v for a, d, v in zip(sums[k], slopes[k], rows_of(flow, step, k))]
        if step:
            s = [v + f for v, f in zip(s, rows_of(stage_f, step))]
    for i, value in enumerate(pulled(sums, [planes[4], planes[5]])):
        grad[i] = value


def descend(kept, got, flow, planes, grad, mine, other):
    steps = flow.shape[0]
    half = mine.shape[2]
    first = lax.rem(lax.axis_index("tm"), 2) == 0
    inverse = 1.0 / (steps / 2)
    s, e, n = prolong_columns(joined(kept, got, 3))
    e, n = e * inverse, n * inverse
    s, e, n = [s, s], inside_x([e, e]), inside_y([n, n])
    face_x, face_y = [planes[0], planes[1]], [planes[2], planes[3]]
    sums = [[jnp.zeros_like(v) for v in s] for _ in range(2)]
    for step in reversed(range(steps)):
        s, e, n, *slopes = fine_step(s, e, n, face_x, face_y)
        for k in range(2):
            sums[k] = [a + d * v for a, d, v in zip(sums[k], slopes[k], rows_of(flow, step, k))]
    total = [grad[i] + v for i, v in enumerate(pulled(sums, [planes[4], planes[5]]))]

    @pl.when(first)
    def _():
        for i in range(2):
            mine[i] = total[i][:, :half]
            other[i] = total[i][:, half:]

    @pl.when(jnp.logical_not(first))
    def _():
        for i in range(2):
            mine[i] = total[i][:, half:]
            other[i] = total[i][:, :half]


def plus(a, b, order, out):
    out[...] = a[...] + b[...]


def weave(mine, other, out, stage, sem):
    first = lax.rem(lax.axis_index("tm"), 2) == 0
    half = stage.shape[1] // 2
    blocks = stage.shape[0] // 2
    for i in range(2):
        left, right = jnp.where(first, mine[i], other[i]), jnp.where(first, other[i], mine[i])
        for v in range(blocks):
            at = slice(v * LANES, (v + 1) * LANES)
            stage[v, pl.ds(i, half, stride=2), :] = left[:, at]
            stage[blocks + v, pl.ds(i, half, stride=2), :] = right[:, at]
    for tile in range(out.shape[0]):
        rows = pl.ds(tile * SUBLANES, SUBLANES)
        pltpu.make_async_copy(stage.at[:, rows], out.at[tile], sem).start()
    wait_all(stage, sem)


def call(body, shapes, operands, *, specs=None, outs=None, scratch=(), cost=1000):
    return pl.pallas_call(
        body,
        out_shape=[jax.ShapeDtypeStruct(shape, jnp.float32) for shape in shapes],
        in_specs=specs or [VMEM] * len(operands),
        out_specs=outs or [VMEM] * len(shapes),
        scratch_shapes=scratch,
        cost_estimate=pl.CostEstimate(flops=cost, bytes_accessed=cost, transcendentals=0),
        compiler_params=pltpu.CompilerParams(vmem_limit_bytes=32 * 1024 * 1024),
    )(*operands)


def in_hbm(value):
    return pltpu.with_memory_space_constraint(value, pltpu.HBM)


def shards(initial, velocity, forcing, depth_table, levels, wet_mask):
    count = lax.axis_size("tm")
    rows, cols = levels.shape
    steps = forcing.shape[0]
    half_rows, half = rows // 2, cols // 4
    halo = -(-count // LANES) * LANES
    width = half + halo
    block = (half_rows, width)
    blocks = cols // LANES
    plane = (half_rows, cols)

    def paired(value, stride):
        return lax.ppermute(value, "tm", [(s, s ^ stride) for s in range(count)])

    def back(value, stride):
        return lax.ppermute(value, "tm", [(s, (s - stride) % count) for s in range(count)])

    def stage(*lead, kind=jnp.float32):
        return pltpu.VMEM((*lead, blocks, rows, LANES), kind)

    tiled_in = dict(levels=levels, wet=wet_mask, initial=initial, forcing=forcing, velocity=velocity)
    tiled_in = {name: in_hbm(tiled(value)) for name, value in tiled_in.items()}
    pinned = in_hbm(initial)
    following = lax.ppermute(initial, "tm", [(s, s - 1) for s in range(1, count)])
    own, sent, planes, coarse_faces = call(
        prepare,
        [(6, *block), (6, *block), (6, *plane), (2, *block)],
        [in_hbm(depth_table), *(tiled_in[name] for name in ("levels", "wet", "initial", "forcing"))],
        specs=[HBM] * 5,
        scratch=[
            pltpu.SMEM(depth_table.shape, jnp.float32),
            stage(kind=jnp.int32),
            stage(kind=jnp.int32),
            stage(3),
            stage(steps),
            pltpu.SemaphoreType.DMA((5,)),
        ],
        cost=PREPARE_COST,
    )
    got = paired(sent, 1)
    (chip,) = call(chip_pair, [(6, *block)], [own, got, coarse_faces])
    per_row = 4 if count <= 16 else 2
    rows_in_all = count // per_row
    if per_row == 4:
        partner = paired(chip, 2)
        row, row_t = call(row_pair, [(6, *block), (3, *block)], [chip, partner, coarse_faces])
    else:
        partner = None
        row, row_t = chip, chip[:3]
    near = back(row, per_row)
    if rows_in_all <= 4:
        far, farther = back(row_t, 2 * per_row), back(row_t, 3 * per_row)
    else:
        stride = 1
        while stride < rows_in_all - 2:
            (row_t,) = call(
                functools.partial(widen, stride, per_row=per_row, rows_in_all=rows_in_all),
                [(3, *block)],
                [row_t, back(row_t, stride * per_row), coarse_faces],
            )
            stride *= 2
        far, farther = back(row_t, 2 * per_row), None

    flow, grad = call(
        base,
        [(steps, 2, blocks, rows, LANES), (2, *plane)],
        [row_t, tiled(following), tiled_in["forcing"], tiled_in["velocity"], planes],
        specs=[ANY, VMEM, HBM, HBM, VMEM],
        scratch=[stage(3), stage(steps), pltpu.SemaphoreType.DMA((3,))],
        cost=BASE_COST,
    )

    operands = {
        "near": near,
        "far": far,
        "farther": farther,
        "own": own,
        "got": got,
        "chip": chip,
        "partner": partner,
        "coarse_faces": coarse_faces,
    }
    names = [name for name, value in operands.items() if value is not None]

    def finish_body(*refs):
        given = dict.fromkeys(operands)
        given.update(zip(names, refs))
        kept, sent = refs[len(names) + 1 :]
        finish(**given, kept=kept, sent=sent, per_row=per_row, rows_in_all=rows_in_all)

    kept, sent = call(
        finish_body,
        [(6, half_rows, half)] * 2,
        [operands[name] for name in names] + [grad],
        specs=[VMEM] * len(names) + [ANY],
    )
    got = paired(sent, 1)
    mine, other = call(
        descend, [(2, half_rows, cols // 2)] * 2, [kept, got, flow, planes, grad], cost=BASE_COST
    )
    mine = mine + paired(other, 1)
    corrected, done = call(
        functools.partial(correct, steps=steps),
        [initial.shape, (8, LANES)],
        [kept, got, pinned],
        specs=[VMEM, VMEM, HBM],
        scratch=[pltpu.VMEM(initial.shape, jnp.float32), pltpu.SemaphoreType.DMA],
        cost=CORRECT_COST,
    )
    if per_row == 4:
        (mine,) = call(plus, [mine.shape], [mine, paired(mine, 2), done], specs=[VMEM, VMEM, ANY])
    if rows_in_all == 4:
        mine = mine + paired(mine, 4) + paired(mine, 8) + paired(mine, 12)
    else:
        stride = per_row
        while stride < count:
            mine = mine + paired(mine, stride)
            stride *= 2
    (gradient,) = call(
        weave,
        [(rows // SUBLANES, blocks, SUBLANES, LANES)],
        [mine, paired(mine, 1)],
        outs=[HBM],
        scratch=[stage(), pltpu.SemaphoreType.DMA],
    )
    return corrected, jnp.swapaxes(gradient, 1, 2).reshape(rows, cols)


def solution(mesh):
    in_specs = (
        P("tm", "parts", None, None),
        P("tm", "parts", None, None),
        P("tm", "parts", None),
        P(),
        P("parts", None),
        P("parts", None),
    )
    out_specs = (P("tm", "parts", None, None), P("parts", None))
    return jax.shard_map(shards, mesh=mesh, in_specs=in_specs, out_specs=out_specs, check_vma=False)
```

```python
import functools

import jax
import jax.numpy as jnp
from jax import lax
from jax.experimental import pallas as pl
from jax.experimental.pallas import tpu as pltpu
from jax.sharding import PartitionSpec as P

COURANT = 0.06
LANES = 128
SUBLANES = 8
VMEM = pl.BlockSpec(memory_space=pltpu.VMEM)
HBM = pl.BlockSpec(memory_space=pltpu.HBM)
ANY = pl.BlockSpec(memory_space=pl.ANY)
PREPARE_COST = 40_000_000
BASE_COST = 8_000_000
CORRECT_COST = 4_000_000
SPLIT_COST = 1000
EXACT = lax.Precision.HIGHEST


def roll(value, steps, axis):
    return pltpu.roll(value, steps % value.shape[axis], axis)


def index_of(shape, axis):
    return lax.broadcasted_iota(jnp.int32, shape, axis)


def faces(depth, scale):
    rows, cols = depth.shape
    half = 0.5 * scale
    east = half * (depth + roll(depth, -1, 1))
    north = half * (depth + roll(depth, -1, 0))
    east = jnp.where(index_of(depth.shape, 1) < cols - 1, east, 0.0)
    north = jnp.where(index_of(depth.shape, 0) < rows - 1, north, 0.0)
    return east, north


def fine_step(s, e, n, face_x, face_y):
    slope_x = [roll(v, -1, 1) - v for v in s]
    slope_y = [s[1] - s[0], roll(s[0], -1, 0) - s[1]]
    e = [v + f * d for v, f, d in zip(e, face_x, slope_x)]
    n = [v + f * d for v, f, d in zip(n, face_y, slope_y)]
    flow_y = [n[0] - roll(n[1], 1, 0), n[1] - n[0]]
    s = [v + ((x - roll(x, 1, 1)) + y) for v, x, y in zip(s, e, flow_y)]
    return s, e, n, slope_x, slope_y


def inside_x(pair):
    cols = pair[0].shape[1]
    keep = index_of(pair[0].shape, 1) < cols - 1
    return [jnp.where(keep, v, 0.0) for v in pair]


def inside_y(pair):
    rows = pair[1].shape[0]
    return [pair[0], jnp.where(index_of(pair[1].shape, 0) < rows - 1, pair[1], 0.0)]


def rows_of(ref, *at):
    half = ref.shape[-2] // 2
    return [
        jnp.concatenate(
            [ref[(*at, v, pl.ds(parity, half, stride=2), slice(None))] for v in range(ref.shape[-3])], axis=1
        )
        for parity in range(2)
    ]


def spread_copies(source, stage, sem):
    lead = (slice(None),) * (len(source.shape) - 4)
    return [
        pltpu.make_async_copy(
            source.at[(*lead, tile)], stage.at[(*lead, slice(None), pl.ds(tile * SUBLANES, SUBLANES))], sem
        )
        for tile in range(source.shape[-4])
    ]


def tiled(value):
    *lead, rows, cols = value.shape
    value = value.reshape(*lead, rows // SUBLANES, SUBLANES, cols // LANES, LANES)
    return jnp.swapaxes(value, -2, -3)


def wait_all(stage, sem):
    pltpu.make_async_copy(stage, stage, sem).wait()


def thirds(value):
    high = value.astype(jnp.bfloat16)
    rest = value - high.astype(jnp.float32)
    mid = rest.astype(jnp.bfloat16)
    low = (rest - mid.astype(jnp.float32)).astype(jnp.bfloat16)
    return jnp.concatenate([high, mid, low], axis=1)


def stacked(fields):
    rows = sum(field.shape[0] for field in fields)
    pad = -rows % 16
    if pad:
        fields = list(fields) + [jnp.zeros((pad, fields[0].shape[1]), jnp.float32)]
    return jnp.concatenate(fields, axis=0)


def restrict_pairs(pairs):
    half, cols = pairs[0][0].shape
    sums = stacked([even + odd for even, odd in pairs])
    gather = pair_matrix((2 * LANES, LANES), 0, 0.25).astype(jnp.bfloat16)
    gather = jnp.concatenate([gather] * 3, axis=0)
    merged = jnp.concatenate(
        [
            jnp.dot(thirds(sums[:, c : c + 2 * LANES]), gather, preferred_element_type=jnp.float32)
            for c in range(0, cols, 2 * LANES)
        ],
        axis=1,
    )
    return [merged[i * half : (i + 1) * half] for i in range(len(pairs))]


def prolong_columns(fields):
    half, cols = fields[0].shape
    rows = stacked(fields)
    spread = pair_matrix((LANES, 2 * LANES), 1, 1.0).astype(jnp.bfloat16)
    spread = jnp.concatenate([spread] * 3, axis=0)
    merged = jnp.concatenate(
        [
            jnp.dot(thirds(rows[:, c : c + LANES]), spread, preferred_element_type=jnp.float32)
            for c in range(0, cols, LANES)
        ],
        axis=1,
    )
    return [merged[i * half : (i + 1) * half] for i in range(len(fields))]


def coarse_step(fields, face_x, face_y):
    return power(fields, 1, face_x, face_y)


def power(fields, count, face_x, face_y):
    if count == 0:
        return fields
    s, e, n = fields
    rows, cols = s.shape
    inner_x = index_of(s.shape, 1) < cols - 1
    inner_y = index_of(s.shape, 0) < rows - 1
    e_in, n_in = jnp.where(inner_x, e, 0.0), jnp.where(inner_y, n, 0.0)
    e_edge, n_edge = e - e_in, n - n_in
    face_x = jnp.where(inner_x, face_x, 0.0)
    face_w, face_s = roll(face_x, 1, 1), roll(face_y, 1, 0)

    def body(_, carried):
        s, e, n, west, south = carried
        e = e + face_x * (roll(s, -1, 1) - s)
        n = n + face_y * (roll(s, -1, 0) - s)
        west = west + face_w * (s - roll(s, 1, 1))
        south = south + face_s * (s - roll(s, 1, 0))
        return s + ((e - west) + (n - south)), e, n, west, south

    carried = (s, e_in, n_in, roll(e_in, 1, 1), roll(n_in, 1, 0))
    if count <= 4:
        for step in range(count):
            carried = body(step, carried)
    else:
        carried = lax.fori_loop(0, count, body, carried)
    s, e, n, _, _ = carried
    return s, e + e_edge, n + n_edge


def add(a, b):
    return tuple(x + y for x, y in zip(a, b))


def scaled(a, factor):
    return tuple(x * factor for x in a)


def pick(first, a, b):
    return tuple(jnp.where(first, x, y) for x, y in zip(a, b))


def read(ref, at=0):
    return tuple(ref[at + i] for i in range(3))


def write(ref, fields, at=0):
    for i, field in enumerate(fields):
        ref[at + i] = field


def pair_matrix(shape, wide_axis, weight):
    wide = index_of(shape, wide_axis) // 2
    return jnp.where(wide == index_of(shape, 1 - wide_axis), weight, 0.0)


def product(a, b):
    return jnp.dot(a, b, precision=EXACT, preferred_element_type=jnp.float32)


def prolong_all(fields):
    half, cols = fields[0].shape
    stacked = jnp.concatenate(fields, axis=0)
    stacked = product(pair_matrix((2 * stacked.shape[0], stacked.shape[0]), 0, 1.0), stacked)
    spread = pair_matrix((LANES, 2 * LANES), 1, 1.0)
    merged = jnp.concatenate(
        [product(stacked[:, c : c + LANES], spread) for c in range(0, cols, LANES)], axis=1
    )
    return [merged[2 * i * half : 2 * (i + 1) * half] for i in range(len(fields))]


def prepare(
    table_in,
    levels,
    wet,
    initial,
    forcing,
    own,
    sent,
    planes,
    window_planes,
    coarse_faces,
    table,
    stage_l,
    stage_w,
    stage_i,
    stage_f,
    sems,
):
    load_table = pltpu.make_async_copy(table_in, table, sems.at[4])
    load_table.start()
    sources = ((levels, stage_l), (wet, stage_w), (initial.at[0], stage_i), (forcing, stage_f))
    for i, (source, stage) in enumerate(sources):
        for copy in spread_copies(source, stage, sems.at[i]):
            copy.start()
    steps = forcing.shape[0]
    width = own.shape[2]
    coarse_cols = stage_l.shape[0] * LANES // 2
    load_table.wait()
    wait_all(stage_l, sems.at[0])
    level = rows_of(stage_l)
    depth = [jnp.zeros(v.shape, jnp.float32) for v in level]
    for i in range(table.shape[0]):
        depth = [jnp.where(v == i, table[i], d) for v, d in zip(level, depth)]
    wait_all(stage_w, sems.at[1])
    dry = [v.astype(jnp.float32) for v in rows_of(stage_w)]
    depth = [d * v for d, v in zip(depth, dry)]
    half = 0.5 * COURANT * COURANT
    face_x = inside_x([half * (d + roll(d, -1, 1)) for d in depth])
    face_y = inside_y([half * (depth[0] + depth[1]), half * (depth[1] + roll(depth[0], -1, 0))])
    all_planes = face_x + face_y + dry
    for i, plane in enumerate(all_planes):
        planes[i] = plane

    wait_all(stage_i, sems.at[2])
    s0 = rows_of(stage_i, 0)
    e0 = [v * COURANT for v in rows_of(stage_i, 1)]
    n0 = [v * COURANT for v in rows_of(stage_i, 2)]
    e_in, n_in = inside_x(e0), inside_y(n0)
    s, e, n = s0, e_in, n_in
    for _ in range(steps):
        s, e, n, _, _ = fine_step(s, e, n, face_x, face_y)
    e = [v + (x - y) for v, x, y in zip(e, e0, e_in)]
    n = [v + (x - y) for v, x, y in zip(n, n0, n_in)]
    relaxed = [s, e, n]

    wait_all(stage_f, sems.at[3])
    s = rows_of(stage_f, steps - 1)
    e = [jnp.zeros_like(v) for v in s]
    n = e
    for step in reversed(range(steps - 1)):
        s, e, n, _, _ = fine_step(s, e, n, face_x, face_y)
        s = [v + f for v, f in zip(s, rows_of(stage_f, step))]
    for pair, start in zip((s, e, n), (s0, e0, n0)):
        relaxed.append([v - x for v, x in zip(pair, start)])
    su, eu, nu, sw, ew, nw, coarse_depth = restrict_pairs(relaxed + [depth])
    ratio = steps / 2
    coarse_courant = COURANT * ratio
    cx, cy = faces(coarse_depth, coarse_courant * coarse_courant)
    w = (sw, ew * ratio, nw * ratio)
    g = add((su, eu * ratio, nu * ratio), coarse_step(w, cx, cy))

    core = lax.rem(lax.axis_index("tm"), 2)
    right = coarse_cols - width
    window = window_planes.shape[2]

    def store(mine, other, start):
        for i, plane in enumerate(all_planes):
            window_planes[i] = plane[:, start : start + window]
        for ref, at in ((own, mine), (sent, other)):
            for i in range(3):
                ref[i] = g[i][:, at : at + width]
                ref[3 + i] = w[i][:, at : at + width]
        coarse_faces[0] = cx[:, mine : mine + width]
        coarse_faces[1] = cy[:, mine : mine + width]

    @pl.when(core == 0)
    def _():
        store(0, right, 0)

    @pl.when(core == 1)
    def _():
        store(right, 0, 2 * coarse_cols - window)


def chip_pair(own, got, coarse_faces, order, out):
    cx, cy = coarse_faces[0], coarse_faces[1]
    first = lax.rem(lax.axis_index("tm"), 2) == 0
    g_own, g_got = read(own), read(got)
    g_low, g_high = pick(first, g_own, g_got), pick(first, g_got, g_own)
    w_low = pick(first, read(own, 3), read(got, 3))
    write(out, add(g_low, coarse_step(g_high, cx, cy)))
    write(out, add(w_low, g_high), 3)


def row_pair(own, got, coarse_faces, order, through, out, out_t, passed):
    cx, cy = coarse_faces[0], coarse_faces[1]
    first = lax.rem(lax.axis_index("tm") // 2, 2) == 0
    t_own, t_got = read(own), read(got)
    t_low, t_high = pick(first, t_own, t_got), pick(first, t_got, t_own)
    q_low = pick(first, read(own, 3), read(got, 3))
    moved = coarse_step(t_high, cx, cy)
    total = add(t_low, coarse_step(moved, cx, cy))
    write(out, total)
    write(out_t, total)
    write(out, add(q_low, moved), 3)


def widen(stride, own, got, coarse_faces, out, *, per_row, rows_in_all):
    row = lax.axis_index("tm") // per_row
    there = jnp.where(row + stride < rows_in_all, 1.0, 0.0)
    moved = power(scaled(read(got), there), per_row * stride, coarse_faces[0], coarse_faces[1])
    write(out, add(read(own), moved))


def finish(near, far, farther, own, got, chip, partner, coarse_faces, starts, kept, sent, *, per_row, rows_in_all):
    cx, cy = coarse_faces[0], coarse_faces[1]
    width = coarse_faces.shape[2]
    half = kept.shape[2]
    device = lax.axis_index("tm")
    row = device // per_row

    def there(stride):
        return jnp.where(row + stride < rows_in_all, 1.0, 0.0)

    rest = scaled(read(far), there(2))
    if farther is not None:
        rest = add(rest, power(scaled(read(farther), there(3)), per_row, cx, cy))
    rest = power(rest, per_row - 1, cx, cy)
    after = add(scaled(read(near, 3), there(1)), rest)
    end = add(scaled(read(near), there(1)), coarse_step(rest, cx, cy))
    if partner is not None:
        low = lax.rem(device // 2, 2) == 0
        moved = coarse_step(end, cx, cy)
        after = pick(low, add(read(partner, 3), moved), after)
        end = pick(low, add(read(partner), coarse_step(moved, cx, cy)), end)
    first = lax.rem(device, 2) == 0
    w_high = pick(first, read(got, 3), read(own, 3))
    q = read(chip, 3)
    c_low = add(q, coarse_step(end, cx, cy))
    c_high = add(w_high, end)

    write(starts, pick(first, c_high, after))
    write(starts, pick(first, after, c_high), 3)

    @pl.when(first)
    def _():
        for i in range(3):
            kept[i] = c_low[i][:, :half]
            sent[i] = c_high[i][:, :half]

    @pl.when(jnp.logical_not(first))
    def _():
        for i in range(3):
            kept[i] = c_high[i][:, width - half :]
            sent[i] = c_low[i][:, width - half :]


def joined(kept, got):
    first = lax.rem(lax.axis_index("tm"), 2) == 0
    fields = []
    for i in range(3):
        left = jnp.where(first, kept[i], got[i])
        right = jnp.where(first, got[i], kept[i])
        fields.append(jnp.concatenate([left, right], axis=1))
    return fields


def correct(kept, got, initial_in, corrected, done, initial, sem, *, steps):
    load = pltpu.make_async_copy(initial_in, initial, sem)
    load.start()
    done[...] = jnp.zeros_like(done)
    unscale = 1.0 / (COURANT * (steps / 2))
    s, e, n = joined(kept, got)
    fields = prolong_all([s, e * unscale, n * unscale])
    load.wait()
    for i, field in enumerate(fields):
        corrected[0, i] = initial[0, i] + field


def pulled(slopes, dry):
    grad_x, grad_y = inside_x(slopes[0]), inside_y(slopes[1])
    across = [grad_y[0] + roll(grad_y[1], 1, 0), grad_y[1] + grad_y[0]]
    return [
        (0.5 * COURANT) * ((x + roll(x, 1, 1)) + y) * keep for x, y, keep in zip(grad_x, across, dry)
    ]


def base(order, following, forcing, velocity, planes, mine, other, stage_i, stage_f, flow, sems):
    sources = ((following.at[0], stage_i), (forcing, stage_f), (velocity, flow))
    for i, (source, stage) in enumerate(sources):
        for copy in spread_copies(source, stage, sems.at[i]):
            copy.start()
    steps = forcing.shape[0]
    device = lax.axis_index("tm")
    there = jnp.where(device + 1 < lax.axis_size("tm"), 1.0, 0.0)
    face_x, face_y = [planes[0], planes[1]], [planes[2], planes[3]]
    wait_all(stage_i, sems.at[0])
    s = [v * there for v in rows_of(stage_i, 0)]
    e = inside_x([v * (there * COURANT) for v in rows_of(stage_i, 1)])
    n = inside_y([v * (there * COURANT) for v in rows_of(stage_i, 2)])
    wait_all(stage_f, sems.at[1])
    wait_all(flow, sems.at[2])
    sums = [[jnp.zeros_like(v) for v in s] for _ in range(2)]
    for step in reversed(range(steps)):
        s, e, n, *slopes = fine_step(s, e, n, face_x, face_y)
        for k in range(2):
            sums[k] = [a + d * v for a, d, v in zip(sums[k], slopes[k], rows_of(flow, step, k))]
        if step:
            s = [v + f for v, f in zip(s, rows_of(stage_f, step))]
    total = pulled(sums, [planes[4], planes[5]])
    first = lax.rem(device, 2) == 0
    half = mine.shape[2]

    @pl.when(first)
    def _():
        for i in range(2):
            mine[i] = total[i][:, :half]
            other[i] = total[i][:, half:]

    @pl.when(jnp.logical_not(first))
    def _():
        for i in range(2):
            mine[i] = total[i][:, half:]
            other[i] = total[i][:, :half]


def split_flow(order, velocity, own, sent, sems):
    core = lax.rem(lax.axis_index("tm"), 2)
    blocks = own.shape[2]
    right = velocity.shape[3] - blocks
    for i, (out, start) in enumerate(((own, core * right), (sent, (1 - core) * right))):
        source = velocity.at[:, :, :, pl.ds(start, blocks)]
        for tile in range(velocity.shape[2]):
            rows = pl.ds(tile * SUBLANES, SUBLANES)
            pltpu.make_async_copy(source.at[:, :, tile], out.at[:, :, :, rows], sems.at[i]).start()
    wait_all(own, sems.at[0])
    wait_all(sent, sems.at[1])


def descend(starts, flow, flow_got, planes, grad, grad_got, mine):
    steps = flow.shape[0]
    half = mine.shape[2]
    width = starts.shape[2]
    window = planes.shape[2]
    first = lax.rem(lax.axis_index("tm"), 2) == 0
    inverse = 1.0 / (steps / 2)
    shift = width - window // 2
    fields = [jnp.where(first, starts[i], roll(starts[i], -shift, 1)) for i in range(6)]
    fields = [field[:, :window] for field in prolong_columns(fields)]
    face_x, face_y = inside_x([planes[0], planes[1]]), [planes[2], planes[3]]
    total = None
    for k, velocity in enumerate((flow, flow_got)):
        s, e, n = fields[3 * k : 3 * k + 3]
        e, n = e * inverse, n * inverse
        s, e, n = [s, s], inside_x([e, e]), inside_y([n, n])
        for step in reversed(range(steps)):
            s, e, n, *slopes = fine_step(s, e, n, face_x, face_y)
            terms = [[d * v for d, v in zip(slopes[i], rows_of(velocity, step, i))] for i in range(2)]
            if total is None:
                total = terms
            else:
                total = [[a + b for a, b in zip(*pair)] for pair in zip(total, terms)]
    total = pulled(total, [planes[4], planes[5]])
    for i in range(2):
        valid = jnp.where(first, total[i][:, :half], total[i][:, window - half :])
        mine[i] = valid + (grad[i] + grad_got[i])


def plus(a, b, order, out):
    out[...] = a[...] + b[...]


def weave(mine, other, out, stage, sem):
    first = lax.rem(lax.axis_index("tm"), 2) == 0
    half = stage.shape[1] // 2
    blocks = stage.shape[0] // 2
    for i in range(2):
        left, right = jnp.where(first, mine[i], other[i]), jnp.where(first, other[i], mine[i])
        for v in range(blocks):
            at = slice(v * LANES, (v + 1) * LANES)
            stage[v, pl.ds(i, half, stride=2), :] = left[:, at]
            stage[blocks + v, pl.ds(i, half, stride=2), :] = right[:, at]
    for tile in range(out.shape[0]):
        rows = pl.ds(tile * SUBLANES, SUBLANES)
        pltpu.make_async_copy(stage.at[:, rows], out.at[tile], sem).start()
    wait_all(stage, sem)


def call(body, shapes, operands, *, specs=None, outs=None, scratch=(), aliases={}, cost=1000):
    return pl.pallas_call(
        body,
        out_shape=[jax.ShapeDtypeStruct(shape, jnp.float32) for shape in shapes],
        in_specs=specs or [VMEM] * len(operands),
        out_specs=outs or [VMEM] * len(shapes),
        scratch_shapes=scratch,
        input_output_aliases=aliases,
        cost_estimate=pl.CostEstimate(flops=cost, bytes_accessed=cost, transcendentals=0),
        compiler_params=pltpu.CompilerParams(vmem_limit_bytes=32 * 1024 * 1024),
    )(*operands)


def in_hbm(value):
    return pltpu.with_memory_space_constraint(value, pltpu.HBM)


def shards(initial, velocity, forcing, depth_table, levels, wet_mask):
    count = lax.axis_size("tm")
    rows, cols = levels.shape
    steps = forcing.shape[0]
    half_rows, half = rows // 2, cols // 4
    halo = -(-count // LANES) * LANES
    width = half + halo
    block = (half_rows, width)
    blocks = cols // LANES
    window = cols // 2 - (-(steps + 1) // LANES) * LANES
    plane = (half_rows, cols)

    def paired(value, stride):
        return lax.ppermute(value, "tm", [(s, s ^ stride) for s in range(count)])

    def back(value, stride):
        return lax.ppermute(value, "tm", [(s, (s - stride) % count) for s in range(count)])

    def stage(*lead, kind=jnp.float32):
        return pltpu.VMEM((*lead, blocks, rows, LANES), kind)

    tiled_in = dict(levels=levels, wet=wet_mask, initial=initial, forcing=forcing, velocity=velocity)
    tiled_in = {name: in_hbm(tiled(value)) for name, value in tiled_in.items()}
    pinned = in_hbm(initial)
    following = lax.ppermute(initial, "tm", [(s, s - 1) for s in range(1, count)])
    own, sent, planes, window_planes, coarse_faces = call(
        prepare,
        [(6, *block), (6, *block), (6, *plane), (6, half_rows, window), (2, *block)],
        [in_hbm(depth_table), *(tiled_in[name] for name in ("levels", "wet", "initial", "forcing"))],
        specs=[HBM] * 5,
        scratch=[
            pltpu.SMEM(depth_table.shape, jnp.float32),
            stage(kind=jnp.int32),
            stage(kind=jnp.int32),
            stage(3),
            stage(steps),
            pltpu.SemaphoreType.DMA((5,)),
        ],
        cost=PREPARE_COST,
    )
    got = paired(sent, 1)
    flow, flow_other = call(
        split_flow,
        [(steps, 2, window // LANES, rows, LANES)] * 2,
        [own, tiled_in["velocity"]],
        specs=[ANY, HBM],
        scratch=[pltpu.SemaphoreType.DMA((2,))],
        cost=SPLIT_COST,
    )
    (chip,) = call(
        chip_pair, [(6, *block)], [own, got, coarse_faces, flow], specs=[VMEM] * 3 + [ANY]
    )
    grad, grad_other = call(
        base,
        [(2, half_rows, cols // 2)] * 2,
        [chip, tiled(following), tiled_in["forcing"], tiled_in["velocity"], planes],
        specs=[ANY, VMEM, HBM, HBM, VMEM],
        scratch=[stage(3), stage(steps), stage(steps, 2), pltpu.SemaphoreType.DMA((3,))],
        cost=BASE_COST,
    )
    per_row = 4 if count <= 16 else 2
    rows_in_all = count // per_row
    if per_row == 4:
        partner = paired(chip, 2)
        row, row_t, flow_other = call(
            row_pair,
            [(6, *block), (3, *block), flow_other.shape],
            [chip, partner, coarse_faces, grad, flow_other],
            specs=[VMEM] * 3 + [ANY] * 2,
            outs=[VMEM] * 2 + [ANY],
            aliases={4: 2},
        )
    else:
        partner = None
        row, row_t = chip, chip[:3]
    near = back(row, per_row)
    if rows_in_all <= 4:
        far, farther = back(row_t, 2 * per_row), back(row_t, 3 * per_row)
    else:
        stride = 1
        while stride < rows_in_all - 2:
            (row_t,) = call(
                functools.partial(widen, stride, per_row=per_row, rows_in_all=rows_in_all),
                [(3, *block)],
                [row_t, back(row_t, stride * per_row), coarse_faces],
            )
            stride *= 2
        far, farther = back(row_t, 2 * per_row), None

    flow_got, grad_got = paired(flow_other, 1), paired(grad_other, 1)

    operands = {
        "near": near,
        "far": far,
        "farther": farther,
        "own": own,
        "got": got,
        "chip": chip,
        "partner": partner,
        "coarse_faces": coarse_faces,
    }
    names = [name for name, value in operands.items() if value is not None]

    def finish_body(*refs):
        given = dict.fromkeys(operands)
        given.update(zip(names, refs))
        starts, kept, sent = refs[len(names) :]
        finish(**given, starts=starts, kept=kept, sent=sent, per_row=per_row, rows_in_all=rows_in_all)

    starts, kept, sent = call(
        finish_body,
        [(6, *block), (3, half_rows, half), (3, half_rows, half)],
        [operands[name] for name in names],
    )
    (mine,) = call(
        descend,
        [(2, half_rows, cols // 2)],
        [starts, flow, flow_got, window_planes, grad, grad_got],
        cost=BASE_COST,
    )
    got = paired(sent, 1)
    corrected, done = call(
        functools.partial(correct, steps=steps),
        [initial.shape, (8, LANES)],
        [kept, got, pinned],
        specs=[VMEM, VMEM, HBM],
        scratch=[pltpu.VMEM(initial.shape, jnp.float32), pltpu.SemaphoreType.DMA],
        cost=CORRECT_COST,
    )
    if per_row == 4:
        (mine,) = call(plus, [mine.shape], [mine, paired(mine, 2), done], specs=[VMEM, VMEM, ANY])
    if rows_in_all == 4:
        mine = mine + paired(mine, 4) + paired(mine, 8) + paired(mine, 12)
    else:
        stride = per_row
        while stride < count:
            mine = mine + paired(mine, stride)
            stride *= 2
    (gradient,) = call(
        weave,
        [(rows // SUBLANES, blocks, SUBLANES, LANES)],
        [mine, paired(mine, 1)],
        outs=[HBM],
        scratch=[stage(), pltpu.SemaphoreType.DMA],
    )
    return corrected, jnp.swapaxes(gradient, 1, 2).reshape(rows, cols)


def solution(mesh):
    in_specs = (
        P("tm", "parts", None, None),
        P("tm", "parts", None, None),
        P("tm", "parts", None),
        P(),
        P("parts", None),
        P("parts", None),
    )
    out_specs = (P("tm", "parts", None, None), P("parts", None))
    return jax.shard_map(shards, mesh=mesh, in_specs=in_specs, out_specs=out_specs, check_vma=False)
```

```python
import functools

import jax
import jax.numpy as jnp
from jax import lax
from jax.experimental import pallas as pl
from jax.experimental.pallas import tpu as pltpu
from jax.sharding import PartitionSpec as P

COURANT = 0.06
LANES = 128
SUBLANES = 8
VMEM = pl.BlockSpec(memory_space=pltpu.VMEM)
HBM = pl.BlockSpec(memory_space=pltpu.HBM)
ANY = pl.BlockSpec(memory_space=pl.ANY)
PREPARE_COST = 40_000_000
BASE_COST = 8_000_000
CORRECT_COST = 4_000_000
SPLIT_COST = 2_000_000
EXACT = lax.Precision.HIGHEST


def roll(value, steps, axis):
    return pltpu.roll(value, steps % value.shape[axis], axis)


def index_of(shape, axis):
    return lax.broadcasted_iota(jnp.int32, shape, axis)


def faces(depth, scale):
    rows, cols = depth.shape
    half = 0.5 * scale
    east = half * (depth + roll(depth, -1, 1))
    north = half * (depth + roll(depth, -1, 0))
    east = jnp.where(index_of(depth.shape, 1) < cols - 1, east, 0.0)
    north = jnp.where(index_of(depth.shape, 0) < rows - 1, north, 0.0)
    return east, north


def fine_step(s, e, n, face_x, face_y):
    slope_x = [roll(v, -1, 1) - v for v in s]
    slope_y = [s[1] - s[0], roll(s[0], -1, 0) - s[1]]
    e = [v + f * d for v, f, d in zip(e, face_x, slope_x)]
    n = [v + f * d for v, f, d in zip(n, face_y, slope_y)]
    flow_y = [n[0] - roll(n[1], 1, 0), n[1] - n[0]]
    s = [v + ((x - roll(x, 1, 1)) + y) for v, x, y in zip(s, e, flow_y)]
    return s, e, n, slope_x, slope_y


def inside_x(pair):
    cols = pair[0].shape[1]
    keep = index_of(pair[0].shape, 1) < cols - 1
    return [jnp.where(keep, v, 0.0) for v in pair]


def inside_y(pair):
    rows = pair[1].shape[0]
    return [pair[0], jnp.where(index_of(pair[1].shape, 0) < rows - 1, pair[1], 0.0)]


def rows_of(ref, *at):
    half = ref.shape[-2] // 2
    return [
        jnp.concatenate(
            [ref[(*at, v, pl.ds(parity, half, stride=2), slice(None))] for v in range(ref.shape[-3])], axis=1
        )
        for parity in range(2)
    ]


def spread_copies(source, stage, sem):
    lead = (slice(None),) * (len(source.shape) - 4)
    return [
        pltpu.make_async_copy(
            source.at[(*lead, tile)], stage.at[(*lead, slice(None), pl.ds(tile * SUBLANES, SUBLANES))], sem
        )
        for tile in range(source.shape[-4])
    ]


def tiled(value):
    *lead, rows, cols = value.shape
    value = value.reshape(*lead, rows // SUBLANES, SUBLANES, cols // LANES, LANES)
    return jnp.swapaxes(value, -2, -3)


def wait_all(stage, sem):
    pltpu.make_async_copy(stage, stage, sem).wait()


def thirds(value):
    high = value.astype(jnp.bfloat16)
    rest = value - high.astype(jnp.float32)
    mid = rest.astype(jnp.bfloat16)
    low = (rest - mid.astype(jnp.float32)).astype(jnp.bfloat16)
    return jnp.concatenate([high, mid, low], axis=1)


def stacked(fields):
    rows = sum(field.shape[0] for field in fields)
    pad = -rows % 16
    if pad:
        fields = list(fields) + [jnp.zeros((pad, fields[0].shape[1]), jnp.float32)]
    return jnp.concatenate(fields, axis=0)


def restrict_pairs(pairs):
    half, cols = pairs[0][0].shape
    sums = stacked([even + odd for even, odd in pairs])
    gather = pair_matrix((2 * LANES, LANES), 0, 0.25).astype(jnp.bfloat16)
    gather = jnp.concatenate([gather] * 3, axis=0)
    merged = jnp.concatenate(
        [
            jnp.dot(thirds(sums[:, c : c + 2 * LANES]), gather, preferred_element_type=jnp.float32)
            for c in range(0, cols, 2 * LANES)
        ],
        axis=1,
    )
    return [merged[i * half : (i + 1) * half] for i in range(len(pairs))]


def prolong_columns(fields):
    half, cols = fields[0].shape
    rows = stacked(fields)
    spread = pair_matrix((LANES, 2 * LANES), 1, 1.0).astype(jnp.bfloat16)
    spread = jnp.concatenate([spread] * 3, axis=0)
    merged = jnp.concatenate(
        [
            jnp.dot(thirds(rows[:, c : c + LANES]), spread, preferred_element_type=jnp.float32)
            for c in range(0, cols, LANES)
        ],
        axis=1,
    )
    return [merged[i * half : (i + 1) * half] for i in range(len(fields))]


def coarse_step(fields, face_x, face_y):
    return power(fields, 1, face_x, face_y)


def power(fields, count, face_x, face_y):
    if count == 0:
        return fields
    s, e, n = fields
    rows, cols = s.shape
    inner_x = index_of(s.shape, 1) < cols - 1
    inner_y = index_of(s.shape, 0) < rows - 1
    e_in, n_in = jnp.where(inner_x, e, 0.0), jnp.where(inner_y, n, 0.0)
    e_edge, n_edge = e - e_in, n - n_in
    face_x = jnp.where(inner_x, face_x, 0.0)
    face_w, face_s = roll(face_x, 1, 1), roll(face_y, 1, 0)

    def body(_, carried):
        s, e, n, west, south = carried
        e = e + face_x * (roll(s, -1, 1) - s)
        n = n + face_y * (roll(s, -1, 0) - s)
        west = west + face_w * (s - roll(s, 1, 1))
        south = south + face_s * (s - roll(s, 1, 0))
        return s + ((e - west) + (n - south)), e, n, west, south

    carried = (s, e_in, n_in, roll(e_in, 1, 1), roll(n_in, 1, 0))
    if count <= 4:
        for step in range(count):
            carried = body(step, carried)
    else:
        carried = lax.fori_loop(0, count, body, carried)
    s, e, n, _, _ = carried
    return s, e + e_edge, n + n_edge


def add(a, b):
    return tuple(x + y for x, y in zip(a, b))


def scaled(a, factor):
    return tuple(x * factor for x in a)


def pick(first, a, b):
    return tuple(jnp.where(first, x, y) for x, y in zip(a, b))


def read(ref, at=0):
    return tuple(ref[at + i] for i in range(3))


def write(ref, fields, at=0):
    for i, field in enumerate(fields):
        ref[at + i] = field


def pair_matrix(shape, wide_axis, weight):
    wide = index_of(shape, wide_axis) // 2
    return jnp.where(wide == index_of(shape, 1 - wide_axis), weight, 0.0)


def product(a, b):
    return jnp.dot(a, b, precision=EXACT, preferred_element_type=jnp.float32)


def prolong_all(fields):
    half, cols = fields[0].shape
    stacked = jnp.concatenate(fields, axis=0)
    stacked = product(pair_matrix((2 * stacked.shape[0], stacked.shape[0]), 0, 1.0), stacked)
    spread = pair_matrix((LANES, 2 * LANES), 1, 1.0)
    merged = jnp.concatenate(
        [product(stacked[:, c : c + LANES], spread) for c in range(0, cols, LANES)], axis=1
    )
    return [merged[2 * i * half : 2 * (i + 1) * half] for i in range(len(fields))]


def prepare(
    table_in,
    levels,
    wet,
    initial,
    forcing,
    own,
    sent,
    planes,
    window_planes,
    coarse_faces,
    table,
    stage_l,
    stage_w,
    stage_i,
    stage_f,
    sems,
):
    load_table = pltpu.make_async_copy(table_in, table, sems.at[4])
    load_table.start()
    sources = ((levels, stage_l), (wet, stage_w), (initial.at[0], stage_i), (forcing, stage_f))
    for i, (source, stage) in enumerate(sources):
        for copy in spread_copies(source, stage, sems.at[i]):
            copy.start()
    steps = forcing.shape[0]
    width = own.shape[2]
    coarse_cols = stage_l.shape[0] * LANES // 2
    load_table.wait()
    wait_all(stage_l, sems.at[0])
    level = rows_of(stage_l)
    depth = [jnp.zeros(v.shape, jnp.float32) for v in level]
    for i in range(table.shape[0]):
        depth = [jnp.where(v == i, table[i], d) for v, d in zip(level, depth)]
    wait_all(stage_w, sems.at[1])
    dry = [v.astype(jnp.float32) for v in rows_of(stage_w)]
    depth = [d * v for d, v in zip(depth, dry)]
    half = 0.5 * COURANT * COURANT
    face_x = inside_x([half * (d + roll(d, -1, 1)) for d in depth])
    face_y = inside_y([half * (depth[0] + depth[1]), half * (depth[1] + roll(depth[0], -1, 0))])
    all_planes = face_x + face_y + dry
    for i, plane in enumerate(all_planes):
        planes[i] = plane

    wait_all(stage_i, sems.at[2])
    s0 = rows_of(stage_i, 0)
    e0 = [v * COURANT for v in rows_of(stage_i, 1)]
    n0 = [v * COURANT for v in rows_of(stage_i, 2)]
    e_in, n_in = inside_x(e0), inside_y(n0)
    s, e, n = s0, e_in, n_in
    for _ in range(steps):
        s, e, n, _, _ = fine_step(s, e, n, face_x, face_y)
    e = [v + (x - y) for v, x, y in zip(e, e0, e_in)]
    n = [v + (x - y) for v, x, y in zip(n, n0, n_in)]
    relaxed = [s, e, n]

    wait_all(stage_f, sems.at[3])
    s = rows_of(stage_f, steps - 1)
    e = [jnp.zeros_like(v) for v in s]
    n = e
    for step in reversed(range(steps - 1)):
        s, e, n, _, _ = fine_step(s, e, n, face_x, face_y)
        s = [v + f for v, f in zip(s, rows_of(stage_f, step))]
    for pair, start in zip((s, e, n), (s0, e0, n0)):
        relaxed.append([v - x for v, x in zip(pair, start)])
    su, eu, nu, sw, ew, nw, coarse_depth = restrict_pairs(relaxed + [depth])
    ratio = steps / 2
    coarse_courant = COURANT * ratio
    cx, cy = faces(coarse_depth, coarse_courant * coarse_courant)
    w = (sw, ew * ratio, nw * ratio)
    g = add((su, eu * ratio, nu * ratio), coarse_step(w, cx, cy))

    core = lax.rem(lax.axis_index("tm"), 2)
    right = coarse_cols - width
    window = window_planes.shape[2]

    def store(mine, other, start):
        for i, plane in enumerate(all_planes):
            window_planes[i] = plane[:, start : start + window]
        for ref, at in ((own, mine), (sent, other)):
            for i in range(3):
                ref[i] = g[i][:, at : at + width]
                ref[3 + i] = w[i][:, at : at + width]
        coarse_faces[0] = cx[:, mine : mine + width]
        coarse_faces[1] = cy[:, mine : mine + width]

    @pl.when(core == 0)
    def _():
        store(0, right, 0)

    @pl.when(core == 1)
    def _():
        store(right, 0, 2 * coarse_cols - window)


def chip_pair(own, got, coarse_faces, out):
    cx, cy = coarse_faces[0], coarse_faces[1]
    first = lax.rem(lax.axis_index("tm"), 2) == 0
    g_own, g_got = read(own), read(got)
    g_low, g_high = pick(first, g_own, g_got), pick(first, g_got, g_own)
    w_low = pick(first, read(own, 3), read(got, 3))
    write(out, add(g_low, coarse_step(g_high, cx, cy)))
    write(out, add(w_low, g_high), 3)


def row_pair(own, got, coarse_faces, order, out, out_t):
    cx, cy = coarse_faces[0], coarse_faces[1]
    first = lax.rem(lax.axis_index("tm") // 2, 2) == 0
    t_own, t_got = read(own), read(got)
    t_low, t_high = pick(first, t_own, t_got), pick(first, t_got, t_own)
    q_low = pick(first, read(own, 3), read(got, 3))
    moved = coarse_step(t_high, cx, cy)
    total = add(t_low, coarse_step(moved, cx, cy))
    write(out, total)
    write(out_t, total)
    write(out, add(q_low, moved), 3)


def widen(stride, own, got, coarse_faces, out, *, per_row, rows_in_all):
    row = lax.axis_index("tm") // per_row
    there = jnp.where(row + stride < rows_in_all, 1.0, 0.0)
    moved = power(scaled(read(got), there), per_row * stride, coarse_faces[0], coarse_faces[1])
    write(out, add(read(own), moved))


def finish(near, far, farther, own, got, chip, partner, coarse_faces, starts, kept, sent, *, per_row, rows_in_all):
    cx, cy = coarse_faces[0], coarse_faces[1]
    width = coarse_faces.shape[2]
    half = kept.shape[2]
    device = lax.axis_index("tm")
    row = device // per_row

    def there(stride):
        return jnp.where(row + stride < rows_in_all, 1.0, 0.0)

    rest = scaled(read(far), there(2))
    if farther is not None:
        rest = add(rest, power(scaled(read(farther), there(3)), per_row, cx, cy))
    rest = power(rest, per_row - 1, cx, cy)
    after = add(scaled(read(near, 3), there(1)), rest)
    end = add(scaled(read(near), there(1)), coarse_step(rest, cx, cy))
    if partner is not None:
        low = lax.rem(device // 2, 2) == 0
        moved = coarse_step(end, cx, cy)
        after = pick(low, add(read(partner, 3), moved), after)
        end = pick(low, add(read(partner), coarse_step(moved, cx, cy)), end)
    first = lax.rem(device, 2) == 0
    w_high = pick(first, read(got, 3), read(own, 3))
    q = read(chip, 3)
    c_low = add(q, coarse_step(end, cx, cy))
    c_high = add(w_high, end)

    write(starts, pick(first, c_high, after))
    write(starts, pick(first, after, c_high), 3)

    @pl.when(first)
    def _():
        for i in range(3):
            kept[i] = c_low[i][:, :half]
            sent[i] = c_high[i][:, :half]

    @pl.when(jnp.logical_not(first))
    def _():
        for i in range(3):
            kept[i] = c_high[i][:, width - half :]
            sent[i] = c_low[i][:, width - half :]


def joined(kept, got):
    first = lax.rem(lax.axis_index("tm"), 2) == 0
    fields = []
    for i in range(3):
        left = jnp.where(first, kept[i], got[i])
        right = jnp.where(first, got[i], kept[i])
        fields.append(jnp.concatenate([left, right], axis=1))
    return fields


def correct(order, kept, got, initial_in, corrected, done, initial, sem, *, steps):
    load = pltpu.make_async_copy(initial_in, initial, sem)
    load.start()
    done[...] = jnp.zeros_like(done)
    unscale = 1.0 / (COURANT * (steps / 2))
    s, e, n = joined(kept, got)
    fields = prolong_all([s, e * unscale, n * unscale])
    load.wait()
    for i, field in enumerate(fields):
        corrected[0, i] = initial[0, i] + field


def pulled(slopes, dry):
    grad_x, grad_y = inside_x(slopes[0]), inside_y(slopes[1])
    across = [grad_y[0] + roll(grad_y[1], 1, 0), grad_y[1] + grad_y[0]]
    return [
        (0.5 * COURANT) * ((x + roll(x, 1, 1)) + y) * keep for x, y, keep in zip(grad_x, across, dry)
    ]


def base(order, following, forcing, velocity, planes, mine, other, stage_i, stage_f, flow, sems):
    sources = ((following.at[0], stage_i), (forcing, stage_f), (velocity, flow))
    for i, (source, stage) in enumerate(sources):
        for copy in spread_copies(source, stage, sems.at[i]):
            copy.start()
    steps = forcing.shape[0]
    device = lax.axis_index("tm")
    there = jnp.where(device + 1 < lax.axis_size("tm"), 1.0, 0.0)
    face_x, face_y = [planes[0], planes[1]], [planes[2], planes[3]]
    wait_all(stage_i, sems.at[0])
    s = [v * there for v in rows_of(stage_i, 0)]
    e = inside_x([v * (there * COURANT) for v in rows_of(stage_i, 1)])
    n = inside_y([v * (there * COURANT) for v in rows_of(stage_i, 2)])
    wait_all(stage_f, sems.at[1])
    wait_all(flow, sems.at[2])
    sums = [[jnp.zeros_like(v) for v in s] for _ in range(2)]
    for step in reversed(range(steps)):
        s, e, n, *slopes = fine_step(s, e, n, face_x, face_y)
        for k in range(2):
            sums[k] = [a + d * v for a, d, v in zip(sums[k], slopes[k], rows_of(flow, step, k))]
        if step:
            s = [v + f for v, f in zip(s, rows_of(stage_f, step))]
    total = pulled(sums, [planes[4], planes[5]])
    first = lax.rem(device, 2) == 0
    half = mine.shape[2]

    @pl.when(first)
    def _():
        for i in range(2):
            mine[i] = total[i][:, :half]
            other[i] = total[i][:, half:]

    @pl.when(jnp.logical_not(first))
    def _():
        for i in range(2):
            mine[i] = total[i][:, half:]
            other[i] = total[i][:, :half]


def cut_flow(order, velocity, velocity_got, own, got, sems):
    blocks = own.shape[2]
    start = lax.rem(lax.axis_index("tm"), 2) * (velocity.shape[3] - blocks)
    for i, (source, out) in enumerate(((velocity, own), (velocity_got, got))):
        source = source.at[:, :, :, pl.ds(start, blocks)]
        for tile in range(velocity.shape[2]):
            rows = pl.ds(tile * SUBLANES, SUBLANES)
            pltpu.make_async_copy(source.at[:, :, tile], out.at[:, :, :, rows], sems.at[i]).start()
    wait_all(own, sems.at[0])
    wait_all(got, sems.at[1])


def descend(starts, flow, flow_got, planes, grad, grad_got, mine):
    steps = flow.shape[0]
    half = mine.shape[2]
    width = starts.shape[2]
    window = planes.shape[2]
    first = lax.rem(lax.axis_index("tm"), 2) == 0
    inverse = 1.0 / (steps / 2)
    shift = width - window // 2
    fields = [jnp.where(first, starts[i], roll(starts[i], -shift, 1)) for i in range(6)]
    fields = [field[:, :window] for field in prolong_columns(fields)]
    face_x, face_y = inside_x([planes[0], planes[1]]), [planes[2], planes[3]]
    total = None
    for k, velocity in enumerate((flow, flow_got)):
        s, e, n = fields[3 * k : 3 * k + 3]
        e, n = e * inverse, n * inverse
        s, e, n = [s, s], inside_x([e, e]), inside_y([n, n])
        for step in reversed(range(steps)):
            s, e, n, *slopes = fine_step(s, e, n, face_x, face_y)
            terms = [[d * v for d, v in zip(slopes[i], rows_of(velocity, step, i))] for i in range(2)]
            if total is None:
                total = terms
            else:
                total = [[a + b for a, b in zip(*pair)] for pair in zip(total, terms)]
    total = pulled(total, [planes[4], planes[5]])
    for i in range(2):
        valid = jnp.where(first, total[i][:, :half], total[i][:, window - half :])
        mine[i] = valid + (grad[i] + grad_got[i])


def plus(a, b, order, out):
    out[...] = a[...] + b[...]


def plus_all(a, b, c, d, order, out):
    out[...] = (a[...] + b[...]) + (c[...] + d[...])


def weave(mine, other, out, stage, sem):
    first = lax.rem(lax.axis_index("tm"), 2) == 0
    half = stage.shape[1] // 2
    blocks = stage.shape[0] // 2
    for i in range(2):
        left, right = jnp.where(first, mine[i], other[i]), jnp.where(first, other[i], mine[i])
        for v in range(blocks):
            at = slice(v * LANES, (v + 1) * LANES)
            stage[v, pl.ds(i, half, stride=2), :] = left[:, at]
            stage[blocks + v, pl.ds(i, half, stride=2), :] = right[:, at]
    for tile in range(out.shape[0]):
        rows = pl.ds(tile * SUBLANES, SUBLANES)
        pltpu.make_async_copy(stage.at[:, rows], out.at[tile], sem).start()
    wait_all(stage, sem)


def call(body, shapes, operands, *, specs=None, outs=None, scratch=(), cost=1000):
    return pl.pallas_call(
        body,
        out_shape=[jax.ShapeDtypeStruct(shape, jnp.float32) for shape in shapes],
        in_specs=specs or [VMEM] * len(operands),
        out_specs=outs or [VMEM] * len(shapes),
        scratch_shapes=scratch,
        cost_estimate=pl.CostEstimate(flops=cost, bytes_accessed=cost, transcendentals=0),
        compiler_params=pltpu.CompilerParams(vmem_limit_bytes=32 * 1024 * 1024),
    )(*operands)


def in_hbm(value):
    return pltpu.with_memory_space_constraint(value, pltpu.HBM)


def shards(initial, velocity, forcing, depth_table, levels, wet_mask):
    count = lax.axis_size("tm")
    rows, cols = levels.shape
    steps = forcing.shape[0]
    half_rows, half = rows // 2, cols // 4
    halo = -(-count // LANES) * LANES
    width = half + halo
    block = (half_rows, width)
    blocks = cols // LANES
    window = cols // 2 - (-(steps + 1) // LANES) * LANES
    plane = (half_rows, cols)

    def paired(value, stride):
        return lax.ppermute(value, "tm", [(s, s ^ stride) for s in range(count)])

    def back(value, stride):
        return lax.ppermute(value, "tm", [(s, (s - stride) % count) for s in range(count)])

    def stage(*lead, kind=jnp.float32):
        return pltpu.VMEM((*lead, blocks, rows, LANES), kind)

    tiled_in = dict(levels=levels, wet=wet_mask, initial=initial, forcing=forcing, velocity=velocity)
    tiled_in = {name: in_hbm(tiled(value)) for name, value in tiled_in.items()}
    pinned = in_hbm(initial)
    velocity_got = paired(velocity, 1)
    following = lax.ppermute(initial, "tm", [(s, s - 1) for s in range(1, count)])
    own, sent, planes, window_planes, coarse_faces = call(
        prepare,
        [(6, *block), (6, *block), (6, *plane), (6, half_rows, window), (2, *block)],
        [in_hbm(depth_table), *(tiled_in[name] for name in ("levels", "wet", "initial", "forcing"))],
        specs=[HBM] * 5,
        scratch=[
            pltpu.SMEM(depth_table.shape, jnp.float32),
            stage(kind=jnp.int32),
            stage(kind=jnp.int32),
            stage(3),
            stage(steps),
            pltpu.SemaphoreType.DMA((5,)),
        ],
        cost=PREPARE_COST,
    )
    got = paired(sent, 1)
    (chip,) = call(
        chip_pair, [(6, *block)], [own, got, coarse_faces]
    )
    grad, grad_other = call(
        base,
        [(2, half_rows, cols // 2)] * 2,
        [chip, tiled(following), tiled_in["forcing"], tiled_in["velocity"], planes],
        specs=[ANY, VMEM, HBM, HBM, VMEM],
        scratch=[stage(3), stage(steps), stage(steps, 2), pltpu.SemaphoreType.DMA((3,))],
        cost=BASE_COST,
    )
    per_row = 4 if count <= 16 else 2
    rows_in_all = count // per_row
    if per_row == 4:
        partner = paired(chip, 2)
        row, row_t = call(
            row_pair,
            [(6, *block), (3, *block)],
            [chip, partner, coarse_faces, grad],
            specs=[VMEM] * 3 + [ANY],
        )
    else:
        partner = None
        row, row_t = chip, chip[:3]
    near = back(row, per_row)
    if rows_in_all <= 4:
        far, farther = back(row_t, 2 * per_row), back(row_t, 3 * per_row)
    else:
        stride = 1
        while stride < rows_in_all - 2:
            (row_t,) = call(
                functools.partial(widen, stride, per_row=per_row, rows_in_all=rows_in_all),
                [(3, *block)],
                [row_t, back(row_t, stride * per_row), coarse_faces],
            )
            stride *= 2
        far, farther = back(row_t, 2 * per_row), None

    grad_got = paired(grad_other, 1)
    flow, flow_got = call(
        cut_flow,
        [(steps, 2, window // LANES, rows, LANES)] * 2,
        [row_t, tiled_in["velocity"], tiled(velocity_got)],
        specs=[ANY, HBM, ANY],
        scratch=[pltpu.SemaphoreType.DMA((2,))],
        cost=SPLIT_COST,
    )

    operands = {
        "near": near,
        "far": far,
        "farther": farther,
        "own": own,
        "got": got,
        "chip": chip,
        "partner": partner,
        "coarse_faces": coarse_faces,
    }
    names = [name for name, value in operands.items() if value is not None]

    def finish_body(*refs):
        given = dict.fromkeys(operands)
        given.update(zip(names, refs))
        starts, kept, sent = refs[len(names) + 1 :]
        finish(**given, starts=starts, kept=kept, sent=sent, per_row=per_row, rows_in_all=rows_in_all)

    starts, kept, sent = call(
        finish_body,
        [(6, *block), (3, half_rows, half), (3, half_rows, half)],
        [operands[name] for name in names] + [flow],
        specs=[VMEM] * len(names) + [ANY],
    )
    (mine,) = call(
        descend,
        [(2, half_rows, cols // 2)],
        [starts, flow, flow_got, window_planes, grad, grad_got],
        cost=BASE_COST,
    )
    got = paired(sent, 1)
    if per_row == 4:
        (mine,) = call(plus, [mine.shape], [mine, paired(mine, 2), got], specs=[VMEM, VMEM, ANY])
    corrected, done = call(
        functools.partial(correct, steps=steps),
        [initial.shape, (8, LANES)],
        [mine, kept, got, pinned],
        specs=[ANY, VMEM, VMEM, HBM],
        scratch=[pltpu.VMEM(initial.shape, jnp.float32), pltpu.SemaphoreType.DMA],
        cost=CORRECT_COST,
    )
    if rows_in_all == 4:
        parts = [mine] + [paired(mine, stride) for stride in (4, 8, 12)]
        (mine,) = call(plus_all, [mine.shape], parts + [done], specs=[VMEM] * 4 + [ANY])
    else:
        stride = per_row
        while stride < count:
            mine = mine + paired(mine, stride)
            stride *= 2
    (gradient,) = call(
        weave,
        [(rows // SUBLANES, blocks, SUBLANES, LANES)],
        [mine, paired(mine, 1)],
        outs=[HBM],
        scratch=[stage(), pltpu.SemaphoreType.DMA],
    )
    return corrected, jnp.swapaxes(gradient, 1, 2).reshape(rows, cols)


def solution(mesh):
    in_specs = (
        P("tm", "parts", None, None),
        P("tm", "parts", None, None),
        P("tm", "parts", None),
        P(),
        P("parts", None),
        P("parts", None),
    )
    out_specs = (P("tm", "parts", None, None), P("parts", None))
    return jax.shard_map(shards, mesh=mesh, in_specs=in_specs, out_specs=out_specs, check_vma=False)
```

```python
import functools

import jax
import jax.numpy as jnp
from jax import lax
from jax.experimental import pallas as pl
from jax.experimental.pallas import tpu as pltpu
from jax.sharding import PartitionSpec as P

COURANT = 0.06
LANES = 128
SUBLANES = 8
VMEM = pl.BlockSpec(memory_space=pltpu.VMEM)
HBM = pl.BlockSpec(memory_space=pltpu.HBM)
ANY = pl.BlockSpec(memory_space=pl.ANY)
PREPARE_COST = 40_000_000
BASE_COST = 8_000_000
CORRECT_COST = 4_000_000
SPLIT_COST = 2_000_000
EXACT = lax.Precision.HIGHEST


def roll(value, steps, axis):
    return pltpu.roll(value, steps % value.shape[axis], axis)


def index_of(shape, axis):
    return lax.broadcasted_iota(jnp.int32, shape, axis)


def faces(depth, scale):
    rows, cols = depth.shape
    half = 0.5 * scale
    east = half * (depth + roll(depth, -1, 1))
    north = half * (depth + roll(depth, -1, 0))
    east = jnp.where(index_of(depth.shape, 1) < cols - 1, east, 0.0)
    north = jnp.where(index_of(depth.shape, 0) < rows - 1, north, 0.0)
    return east, north


def fine_step(s, e, n, face_x, face_y):
    slope_x = [roll(v, -1, 1) - v for v in s]
    slope_y = [s[1] - s[0], roll(s[0], -1, 0) - s[1]]
    e = [v + f * d for v, f, d in zip(e, face_x, slope_x)]
    n = [v + f * d for v, f, d in zip(n, face_y, slope_y)]
    flow_y = [n[0] - roll(n[1], 1, 0), n[1] - n[0]]
    s = [v + ((x - roll(x, 1, 1)) + y) for v, x, y in zip(s, e, flow_y)]
    return s, e, n, slope_x, slope_y


def inside_x(pair):
    cols = pair[0].shape[1]
    keep = index_of(pair[0].shape, 1) < cols - 1
    return [jnp.where(keep, v, 0.0) for v in pair]


def inside_y(pair):
    rows = pair[1].shape[0]
    return [pair[0], jnp.where(index_of(pair[1].shape, 0) < rows - 1, pair[1], 0.0)]


def rows_of(ref, *at, first=0, blocks=None):
    half = ref.shape[-2] // 2
    return [
        jnp.concatenate(
            [
                ref[(*at, first + v, pl.ds(parity, half, stride=2), slice(None))]
                for v in range(blocks or ref.shape[-3])
            ],
            axis=1,
        )
        for parity in range(2)
    ]


def spread_copies(source, stage, sem):
    lead = (slice(None),) * (len(source.shape) - 4)
    return [
        pltpu.make_async_copy(
            source.at[(*lead, tile)], stage.at[(*lead, slice(None), pl.ds(tile * SUBLANES, SUBLANES))], sem
        )
        for tile in range(source.shape[-4])
    ]


def tiled(value):
    *lead, rows, cols = value.shape
    value = value.reshape(*lead, rows // SUBLANES, SUBLANES, cols // LANES, LANES)
    return jnp.swapaxes(value, -2, -3)


def wait_all(stage, sem):
    pltpu.make_async_copy(stage, stage, sem).wait()


def thirds(value):
    high = value.astype(jnp.bfloat16)
    rest = value - high.astype(jnp.float32)
    mid = rest.astype(jnp.bfloat16)
    low = (rest - mid.astype(jnp.float32)).astype(jnp.bfloat16)
    return jnp.concatenate([high, mid, low], axis=1)


def stacked(fields):
    rows = sum(field.shape[0] for field in fields)
    pad = -rows % 16
    if pad:
        fields = list(fields) + [jnp.zeros((pad, fields[0].shape[1]), jnp.float32)]
    return jnp.concatenate(fields, axis=0)


def restrict_pairs(pairs):
    half, cols = pairs[0][0].shape
    sums = stacked([even + odd for even, odd in pairs])
    gather = pair_matrix((2 * LANES, LANES), 0, 0.25).astype(jnp.bfloat16)
    gather = jnp.concatenate([gather] * 3, axis=0)
    merged = jnp.concatenate(
        [
            jnp.dot(thirds(sums[:, c : c + 2 * LANES]), gather, preferred_element_type=jnp.float32)
            for c in range(0, cols, 2 * LANES)
        ],
        axis=1,
    )
    return [merged[i * half : (i + 1) * half] for i in range(len(pairs))]


def prolong_columns(fields):
    half, cols = fields[0].shape
    rows = stacked(fields)
    spread = pair_matrix((LANES, 2 * LANES), 1, 1.0).astype(jnp.bfloat16)
    spread = jnp.concatenate([spread] * 3, axis=0)
    merged = jnp.concatenate(
        [
            jnp.dot(thirds(rows[:, c : c + LANES]), spread, preferred_element_type=jnp.float32)
            for c in range(0, cols, LANES)
        ],
        axis=1,
    )
    return [merged[i * half : (i + 1) * half] for i in range(len(fields))]


def coarse_step(fields, face_x, face_y):
    return power(fields, 1, face_x, face_y)


def power(fields, count, face_x, face_y):
    if count == 0:
        return fields
    s, e, n = fields
    rows, cols = s.shape
    inner_x = index_of(s.shape, 1) < cols - 1
    inner_y = index_of(s.shape, 0) < rows - 1
    e_in, n_in = jnp.where(inner_x, e, 0.0), jnp.where(inner_y, n, 0.0)
    e_edge, n_edge = e - e_in, n - n_in
    face_x = jnp.where(inner_x, face_x, 0.0)
    face_w, face_s = roll(face_x, 1, 1), roll(face_y, 1, 0)

    def body(_, carried):
        s, e, n, west, south = carried
        e = e + face_x * (roll(s, -1, 1) - s)
        n = n + face_y * (roll(s, -1, 0) - s)
        west = west + face_w * (s - roll(s, 1, 1))
        south = south + face_s * (s - roll(s, 1, 0))
        return s + ((e - west) + (n - south)), e, n, west, south

    carried = (s, e_in, n_in, roll(e_in, 1, 1), roll(n_in, 1, 0))
    if count <= 4:
        for step in range(count):
            carried = body(step, carried)
    else:
        carried = lax.fori_loop(0, count, body, carried)
    s, e, n, _, _ = carried
    return s, e + e_edge, n + n_edge


def add(a, b):
    return tuple(x + y for x, y in zip(a, b))


def scaled(a, factor):
    return tuple(x * factor for x in a)


def pick(first, a, b):
    return tuple(jnp.where(first, x, y) for x, y in zip(a, b))


def read(ref, at=0):
    return tuple(ref[at + i] for i in range(3))


def write(ref, fields, at=0):
    for i, field in enumerate(fields):
        ref[at + i] = field


def pair_matrix(shape, wide_axis, weight):
    wide = index_of(shape, wide_axis) // 2
    return jnp.where(wide == index_of(shape, 1 - wide_axis), weight, 0.0)


def product(a, b):
    return jnp.dot(a, b, precision=EXACT, preferred_element_type=jnp.float32)


def prolong_all(fields):
    half, cols = fields[0].shape
    stacked = jnp.concatenate(fields, axis=0)
    stacked = product(pair_matrix((2 * stacked.shape[0], stacked.shape[0]), 0, 1.0), stacked)
    spread = pair_matrix((LANES, 2 * LANES), 1, 1.0)
    merged = jnp.concatenate(
        [product(stacked[:, c : c + LANES], spread) for c in range(0, cols, LANES)], axis=1
    )
    return [merged[2 * i * half : 2 * (i + 1) * half] for i in range(len(fields))]


def prepare(
    table_in,
    levels,
    wet,
    initial,
    forcing,
    velocity,
    own,
    sent,
    planes,
    window_planes,
    coarse_faces,
    stage_f,
    flow,
    table,
    stage_l,
    stage_w,
    stage_i,
    sems,
):
    load_table = pltpu.make_async_copy(table_in, table, sems.at[5])
    load_table.start()
    sources = ((levels, stage_l), (wet, stage_w), (initial.at[0], stage_i), (forcing, stage_f), (velocity, flow))
    for i, (source, stage) in enumerate(sources):
        for copy in spread_copies(source, stage, sems.at[i]):
            copy.start()
    steps = forcing.shape[0]
    width = own.shape[2]
    coarse_cols = stage_l.shape[0] * LANES // 2
    load_table.wait()
    wait_all(stage_l, sems.at[0])
    level = rows_of(stage_l)
    depth = [jnp.zeros(v.shape, jnp.float32) for v in level]
    for i in range(table.shape[0]):
        depth = [jnp.where(v == i, table[i], d) for v, d in zip(level, depth)]
    wait_all(stage_w, sems.at[1])
    dry = [v.astype(jnp.float32) for v in rows_of(stage_w)]
    depth = [d * v for d, v in zip(depth, dry)]
    half = 0.5 * COURANT * COURANT
    face_x = inside_x([half * (d + roll(d, -1, 1)) for d in depth])
    face_y = inside_y([half * (depth[0] + depth[1]), half * (depth[1] + roll(depth[0], -1, 0))])
    all_planes = face_x + face_y + dry
    for i, plane in enumerate(all_planes):
        planes[i] = plane

    wait_all(stage_i, sems.at[2])
    s0 = rows_of(stage_i, 0)
    e0 = [v * COURANT for v in rows_of(stage_i, 1)]
    n0 = [v * COURANT for v in rows_of(stage_i, 2)]
    e_in, n_in = inside_x(e0), inside_y(n0)
    s, e, n = s0, e_in, n_in
    for _ in range(steps):
        s, e, n, _, _ = fine_step(s, e, n, face_x, face_y)
    e = [v + (x - y) for v, x, y in zip(e, e0, e_in)]
    n = [v + (x - y) for v, x, y in zip(n, n0, n_in)]
    relaxed = [s, e, n]

    wait_all(stage_f, sems.at[3])
    s = rows_of(stage_f, steps - 1)
    e = [jnp.zeros_like(v) for v in s]
    n = e
    for step in reversed(range(steps - 1)):
        s, e, n, _, _ = fine_step(s, e, n, face_x, face_y)
        s = [v + f for v, f in zip(s, rows_of(stage_f, step))]
    for pair, start in zip((s, e, n), (s0, e0, n0)):
        relaxed.append([v - x for v, x in zip(pair, start)])
    su, eu, nu, sw, ew, nw, coarse_depth = restrict_pairs(relaxed + [depth])
    ratio = steps / 2
    coarse_courant = COURANT * ratio
    cx, cy = faces(coarse_depth, coarse_courant * coarse_courant)
    w = (sw, ew * ratio, nw * ratio)
    g = add((su, eu * ratio, nu * ratio), coarse_step(w, cx, cy))

    core = lax.rem(lax.axis_index("tm"), 2)
    right = coarse_cols - width
    window = window_planes.shape[2]

    def store(mine, other, start):
        for i, plane in enumerate(all_planes):
            window_planes[i] = plane[:, start : start + window]
        for ref, at in ((own, mine), (sent, other)):
            for i in range(3):
                ref[i] = g[i][:, at : at + width]
                ref[3 + i] = w[i][:, at : at + width]
        coarse_faces[0] = cx[:, mine : mine + width]
        coarse_faces[1] = cy[:, mine : mine + width]

    @pl.when(core == 0)
    def _():
        store(0, right, 0)

    @pl.when(core == 1)
    def _():
        store(right, 0, 2 * coarse_cols - window)

    wait_all(flow, sems.at[4])


def chip_pair(own, got, coarse_faces, out):
    cx, cy = coarse_faces[0], coarse_faces[1]
    first = lax.rem(lax.axis_index("tm"), 2) == 0
    g_own, g_got = read(own), read(got)
    g_low, g_high = pick(first, g_own, g_got), pick(first, g_got, g_own)
    w_low = pick(first, read(own, 3), read(got, 3))
    write(out, add(g_low, coarse_step(g_high, cx, cy)))
    write(out, add(w_low, g_high), 3)


def row_pair(own, got, coarse_faces, order, out, out_t):
    cx, cy = coarse_faces[0], coarse_faces[1]
    first = lax.rem(lax.axis_index("tm") // 2, 2) == 0
    t_own, t_got = read(own), read(got)
    t_low, t_high = pick(first, t_own, t_got), pick(first, t_got, t_own)
    q_low = pick(first, read(own, 3), read(got, 3))
    moved = coarse_step(t_high, cx, cy)
    total = add(t_low, coarse_step(moved, cx, cy))
    write(out, total)
    write(out_t, total)
    write(out, add(q_low, moved), 3)


def widen(stride, own, got, coarse_faces, out, *, per_row, rows_in_all):
    row = lax.axis_index("tm") // per_row
    there = jnp.where(row + stride < rows_in_all, 1.0, 0.0)
    moved = power(scaled(read(got), there), per_row * stride, coarse_faces[0], coarse_faces[1])
    write(out, add(read(own), moved))


def finish(near, far, farther, own, got, chip, partner, coarse_faces, starts, kept, sent, *, per_row, rows_in_all):
    cx, cy = coarse_faces[0], coarse_faces[1]
    width = coarse_faces.shape[2]
    half = kept.shape[2]
    device = lax.axis_index("tm")
    row = device // per_row

    def there(stride):
        return jnp.where(row + stride < rows_in_all, 1.0, 0.0)

    rest = scaled(read(far), there(2))
    if farther is not None:
        rest = add(rest, power(scaled(read(farther), there(3)), per_row, cx, cy))
    rest = power(rest, per_row - 1, cx, cy)
    after = add(scaled(read(near, 3), there(1)), rest)
    end = add(scaled(read(near), there(1)), coarse_step(rest, cx, cy))
    if partner is not None:
        low = lax.rem(device // 2, 2) == 0
        moved = coarse_step(end, cx, cy)
        after = pick(low, add(read(partner, 3), moved), after)
        end = pick(low, add(read(partner), coarse_step(moved, cx, cy)), end)
    first = lax.rem(device, 2) == 0
    w_high = pick(first, read(got, 3), read(own, 3))
    q = read(chip, 3)
    c_low = add(q, coarse_step(end, cx, cy))
    c_high = add(w_high, end)

    write(starts, pick(first, c_high, after))
    write(starts, pick(first, after, c_high), 3)

    @pl.when(first)
    def _():
        for i in range(3):
            kept[i] = c_low[i][:, :half]
            sent[i] = c_high[i][:, :half]

    @pl.when(jnp.logical_not(first))
    def _():
        for i in range(3):
            kept[i] = c_high[i][:, width - half :]
            sent[i] = c_low[i][:, width - half :]


def joined(kept, got):
    first = lax.rem(lax.axis_index("tm"), 2) == 0
    fields = []
    for i in range(3):
        left = jnp.where(first, kept[i], got[i])
        right = jnp.where(first, got[i], kept[i])
        fields.append(jnp.concatenate([left, right], axis=1))
    return fields


def correct(order, kept, got, initial_in, corrected, done, initial, sem, *, steps):
    load = pltpu.make_async_copy(initial_in, initial, sem)
    load.start()
    done[...] = jnp.zeros_like(done)
    unscale = 1.0 / (COURANT * (steps / 2))
    s, e, n = joined(kept, got)
    fields = prolong_all([s, e * unscale, n * unscale])
    load.wait()
    for i, field in enumerate(fields):
        corrected[0, i] = initial[0, i] + field


def pulled(slopes, dry):
    grad_x, grad_y = inside_x(slopes[0]), inside_y(slopes[1])
    across = [grad_y[0] + roll(grad_y[1], 1, 0), grad_y[1] + grad_y[0]]
    return [
        (0.5 * COURANT) * ((x + roll(x, 1, 1)) + y) * keep for x, y, keep in zip(grad_x, across, dry)
    ]


def base(order, following, stage_f, flow, planes, mine, other, stage_i, sem):
    for copy in spread_copies(following.at[0], stage_i, sem):
        copy.start()
    steps = flow.shape[0]
    device = lax.axis_index("tm")
    there = jnp.where(device + 1 < lax.axis_size("tm"), 1.0, 0.0)
    face_x, face_y = [planes[0], planes[1]], [planes[2], planes[3]]
    wait_all(stage_i, sem)
    s = [v * there for v in rows_of(stage_i, 0)]
    e = inside_x([v * (there * COURANT) for v in rows_of(stage_i, 1)])
    n = inside_y([v * (there * COURANT) for v in rows_of(stage_i, 2)])
    sums = [[jnp.zeros_like(v) for v in s] for _ in range(2)]
    for step in reversed(range(steps)):
        s, e, n, *slopes = fine_step(s, e, n, face_x, face_y)
        for k in range(2):
            sums[k] = [a + d * v for a, d, v in zip(sums[k], slopes[k], rows_of(flow, step, k))]
        if step:
            s = [v + f for v, f in zip(s, rows_of(stage_f, step))]
    total = pulled(sums, [planes[4], planes[5]])
    first = lax.rem(device, 2) == 0
    half = mine.shape[2]

    @pl.when(first)
    def _():
        for i in range(2):
            mine[i] = total[i][:, :half]
            other[i] = total[i][:, half:]

    @pl.when(jnp.logical_not(first))
    def _():
        for i in range(2):
            mine[i] = total[i][:, half:]
            other[i] = total[i][:, :half]


def cut_flow(order, velocity, out, sem):
    blocks = out.shape[2]
    start = lax.rem(lax.axis_index("tm"), 2) * (velocity.shape[3] - blocks)
    for copy in spread_copies(velocity.at[:, :, :, pl.ds(start, blocks)], out, sem):
        copy.start()
    wait_all(out, sem)


def descend(starts, flow, flow_got, planes, grad, grad_got, mine):
    steps = flow.shape[0]
    half = mine.shape[2]
    width = starts.shape[2]
    window = planes.shape[2]
    first = lax.rem(lax.axis_index("tm"), 2) == 0
    inverse = 1.0 / (steps / 2)
    shift = width - window // 2
    fields = [jnp.where(first, starts[i], roll(starts[i], -shift, 1)) for i in range(6)]
    fields = [field[:, :window] for field in prolong_columns(fields)]
    face_x, face_y = inside_x([planes[0], planes[1]]), [planes[2], planes[3]]
    total = None
    blocks = flow_got.shape[2]
    start = jnp.where(first, 0, flow.shape[2] - blocks)
    for k, (velocity, at) in enumerate(((flow, start), (flow_got, 0))):
        s, e, n = fields[3 * k : 3 * k + 3]
        e, n = e * inverse, n * inverse
        s, e, n = [s, s], inside_x([e, e]), inside_y([n, n])
        for step in reversed(range(steps)):
            s, e, n, *slopes = fine_step(s, e, n, face_x, face_y)
            terms = [[d * v for d, v in zip(slopes[i], rows_of(velocity, step, i, first=at, blocks=blocks))] for i in range(2)]
            if total is None:
                total = terms
            else:
                total = [[a + b for a, b in zip(*pair)] for pair in zip(total, terms)]
    total = pulled(total, [planes[4], planes[5]])
    for i in range(2):
        valid = jnp.where(first, total[i][:, :half], total[i][:, window - half :])
        mine[i] = valid + (grad[i] + grad_got[i])


def plus(a, b, order, out):
    out[...] = a[...] + b[...]


def plus_all(a, b, c, d, order, out):
    out[...] = (a[...] + b[...]) + (c[...] + d[...])


def weave(mine, other, out, stage, sem):
    first = lax.rem(lax.axis_index("tm"), 2) == 0
    half = stage.shape[1] // 2
    blocks = stage.shape[0] // 2
    for i in range(2):
        left, right = jnp.where(first, mine[i], other[i]), jnp.where(first, other[i], mine[i])
        for v in range(blocks):
            at = slice(v * LANES, (v + 1) * LANES)
            stage[v, pl.ds(i, half, stride=2), :] = left[:, at]
            stage[blocks + v, pl.ds(i, half, stride=2), :] = right[:, at]
    for tile in range(out.shape[0]):
        rows = pl.ds(tile * SUBLANES, SUBLANES)
        pltpu.make_async_copy(stage.at[:, rows], out.at[tile], sem).start()
    wait_all(stage, sem)


def call(body, shapes, operands, *, specs=None, outs=None, scratch=(), cost=1000):
    return pl.pallas_call(
        body,
        out_shape=[jax.ShapeDtypeStruct(shape, jnp.float32) for shape in shapes],
        in_specs=specs or [VMEM] * len(operands),
        out_specs=outs or [VMEM] * len(shapes),
        scratch_shapes=scratch,
        cost_estimate=pl.CostEstimate(flops=cost, bytes_accessed=cost, transcendentals=0),
        compiler_params=pltpu.CompilerParams(vmem_limit_bytes=32 * 1024 * 1024),
    )(*operands)


def in_hbm(value):
    return pltpu.with_memory_space_constraint(value, pltpu.HBM)


def shards(initial, velocity, forcing, depth_table, levels, wet_mask):
    count = lax.axis_size("tm")
    rows, cols = levels.shape
    steps = forcing.shape[0]
    half_rows, half = rows // 2, cols // 4
    halo = -(-count // LANES) * LANES
    width = half + halo
    block = (half_rows, width)
    blocks = cols // LANES
    window = cols // 2 - (-(steps + 1) // LANES) * LANES
    plane = (half_rows, cols)

    def paired(value, stride):
        return lax.ppermute(value, "tm", [(s, s ^ stride) for s in range(count)])

    def back(value, stride):
        return lax.ppermute(value, "tm", [(s, (s - stride) % count) for s in range(count)])

    def stage(*lead, kind=jnp.float32):
        return pltpu.VMEM((*lead, blocks, rows, LANES), kind)

    tiled_in = dict(levels=levels, wet=wet_mask, initial=initial, forcing=forcing, velocity=velocity)
    tiled_in = {name: in_hbm(tiled(value)) for name, value in tiled_in.items()}
    pinned = in_hbm(initial)
    velocity_got = paired(velocity, 1)
    following = lax.ppermute(initial, "tm", [(s, s - 1) for s in range(1, count)])
    own, sent, planes, window_planes, coarse_faces, staged_forcing, flow = call(
        prepare,
        [
            (6, *block),
            (6, *block),
            (6, *plane),
            (6, half_rows, window),
            (2, *block),
            (steps, blocks, rows, LANES),
            (steps, 2, blocks, rows, LANES),
        ],
        [in_hbm(depth_table), *(tiled_in[name] for name in ("levels", "wet", "initial", "forcing", "velocity"))],
        specs=[HBM] * 6,
        scratch=[
            pltpu.SMEM(depth_table.shape, jnp.float32),
            stage(kind=jnp.int32),
            stage(kind=jnp.int32),
            stage(3),
            pltpu.SemaphoreType.DMA((6,)),
        ],
        cost=PREPARE_COST,
    )
    got = paired(sent, 1)
    (chip,) = call(
        chip_pair, [(6, *block)], [own, got, coarse_faces]
    )
    grad, grad_other = call(
        base,
        [(2, half_rows, cols // 2)] * 2,
        [chip, tiled(following), staged_forcing, flow, planes],
        specs=[ANY] + [VMEM] * 4,
        scratch=[stage(3), pltpu.SemaphoreType.DMA],
        cost=BASE_COST,
    )
    grad_got = paired(grad_other, 1)
    per_row = 4 if count <= 16 else 2
    rows_in_all = count // per_row
    if per_row == 4:
        partner = paired(chip, 2)
        row, row_t = call(
            row_pair,
            [(6, *block), (3, *block)],
            [chip, partner, coarse_faces, grad_got],
            specs=[VMEM] * 3 + [ANY],
        )
    else:
        partner = None
        row, row_t = chip, chip[:3]
    near = back(row, per_row)
    if rows_in_all <= 4:
        far, farther = back(row_t, 2 * per_row), back(row_t, 3 * per_row)
    else:
        stride = 1
        while stride < rows_in_all - 2:
            (row_t,) = call(
                functools.partial(widen, stride, per_row=per_row, rows_in_all=rows_in_all),
                [(3, *block)],
                [row_t, back(row_t, stride * per_row), coarse_faces],
            )
            stride *= 2
        far, farther = back(row_t, 2 * per_row), None

    (flow_got,) = call(
        cut_flow,
        [(steps, 2, window // LANES, rows, LANES)],
        [row_t, tiled(velocity_got)],
        specs=[ANY, ANY],
        scratch=[pltpu.SemaphoreType.DMA],
        cost=SPLIT_COST,
    )

    operands = {
        "near": near,
        "far": far,
        "farther": farther,
        "own": own,
        "got": got,
        "chip": chip,
        "partner": partner,
        "coarse_faces": coarse_faces,
    }
    names = [name for name, value in operands.items() if value is not None]

    def finish_body(*refs):
        given = dict.fromkeys(operands)
        given.update(zip(names, refs))
        starts, kept, sent = refs[len(names) + 1 :]
        finish(**given, starts=starts, kept=kept, sent=sent, per_row=per_row, rows_in_all=rows_in_all)

    starts, kept, sent = call(
        finish_body,
        [(6, *block), (3, half_rows, half), (3, half_rows, half)],
        [operands[name] for name in names] + [flow_got],
        specs=[VMEM] * len(names) + [ANY],
    )
    (mine,) = call(
        descend,
        [(2, half_rows, cols // 2)],
        [starts, flow, flow_got, window_planes, grad, grad_got],
        cost=BASE_COST,
    )
    got = paired(sent, 1)
    if per_row == 4:
        (mine,) = call(plus, [mine.shape], [mine, paired(mine, 2), got], specs=[VMEM, VMEM, ANY])
    corrected, done = call(
        functools.partial(correct, steps=steps),
        [initial.shape, (8, LANES)],
        [mine, kept, got, pinned],
        specs=[ANY, VMEM, VMEM, HBM],
        scratch=[pltpu.VMEM(initial.shape, jnp.float32), pltpu.SemaphoreType.DMA],
        cost=CORRECT_COST,
    )
    if rows_in_all == 4:
        parts = [mine] + [paired(mine, stride) for stride in (4, 8, 12)]
        (mine,) = call(plus_all, [mine.shape], parts + [done], specs=[VMEM] * 4 + [ANY])
    else:
        stride = per_row
        while stride < count:
            mine = mine + paired(mine, stride)
            stride *= 2
    (gradient,) = call(
        weave,
        [(rows // SUBLANES, blocks, SUBLANES, LANES)],
        [mine, paired(mine, 1)],
        outs=[HBM],
        scratch=[stage(), pltpu.SemaphoreType.DMA],
    )
    return corrected, jnp.swapaxes(gradient, 1, 2).reshape(rows, cols)


def solution(mesh):
    in_specs = (
        P("tm", "parts", None, None),
        P("tm", "parts", None, None),
        P("tm", "parts", None),
        P(),
        P("parts", None),
        P("parts", None),
    )
    out_specs = (P("tm", "parts", None, None), P("parts", None))
    return jax.shard_map(shards, mesh=mesh, in_specs=in_specs, out_specs=out_specs, check_vma=False)
```

```python
import functools

import jax
import jax.numpy as jnp
from jax import lax
from jax.experimental import pallas as pl
from jax.experimental.pallas import tpu as pltpu
from jax.sharding import PartitionSpec as P

COURANT = 0.06
LANES = 128
SUBLANES = 8
VMEM = pl.BlockSpec(memory_space=pltpu.VMEM)
HBM = pl.BlockSpec(memory_space=pltpu.HBM)
ANY = pl.BlockSpec(memory_space=pl.ANY)
PREPARE_COST = 40_000_000
BASE_COST = 8_000_000
CORRECT_COST = 4_000_000
SPLIT_COST = 2_000_000
EXACT = lax.Precision.HIGHEST


def roll(value, steps, axis):
    return pltpu.roll(value, steps % value.shape[axis], axis)


def index_of(shape, axis):
    return lax.broadcasted_iota(jnp.int32, shape, axis)


def faces(depth, scale):
    rows, cols = depth.shape
    half = 0.5 * scale
    east = half * (depth + roll(depth, -1, 1))
    north = half * (depth + roll(depth, -1, 0))
    east = jnp.where(index_of(depth.shape, 1) < cols - 1, east, 0.0)
    north = jnp.where(index_of(depth.shape, 0) < rows - 1, north, 0.0)
    return east, north


def fine_step(s, e, n, face_x, face_y, forcing=None, flow=None, sums=None):
    lane = index_of(s[0][0].shape, 1)
    count = len(s[0])
    new_s, new_e, new_n = ([[], []] for _ in range(3))
    turned = [roll(p[0], -1, 1) for p in s]
    west = [0.0, 0.0]
    for v in range(count):
        here = [p[v] for p in s]
        ahead = [roll(p[min(v + 1, count - 1)], -1, 1) for p in s]
        slope_x = [jnp.where(lane < LANES - 1, t, a) - h for t, a, h in zip(turned, ahead, here)]
        slope_y = [here[1] - here[0], roll(here[0], -1, 0) - here[1]]
        turned = ahead
        east = [e[p][v] + face_x[p][v] * slope_x[p] for p in range(2)]
        north = [n[p][v] + face_y[p][v] * slope_y[p] for p in range(2)]
        flow_y = [north[0] - roll(north[1], 1, 0), north[1] - north[0]]
        back = [roll(x, 1, 1) for x in east]
        for p in range(2):
            value = here[p] + ((east[p] - jnp.where(lane > 0, back[p], west[p])) + flow_y[p])
            if forcing is not None:
                value = value + forcing(p, v)
            new_s[p].append(value)
            new_e[p].append(east[p])
            new_n[p].append(north[p])
            if flow is not None:
                for k, slope in enumerate((slope_x, slope_y)):
                    term = slope[p] * flow(k, p, v)
                    if len(sums[k][p]) > v:
                        sums[k][p][v] = sums[k][p][v] + term
                    else:
                        sums[k][p].append(term)
        west = back
    return new_s, new_e, new_n


def cut(*pairs):
    return [[[v[:, c : c + LANES] for c in range(0, v.shape[1], LANES)] for v in pair] for pair in pairs]


def glued(*pairs):
    return [[jnp.concatenate(blocks, axis=1) for blocks in pair] for pair in pairs]


def block_of(ref, *at, parity):
    return ref[(*at, pl.ds(parity, ref.shape[-2] // 2, stride=2), slice(None))]


def inside_x(pair):
    cols = pair[0].shape[1]
    keep = index_of(pair[0].shape, 1) < cols - 1
    return [jnp.where(keep, v, 0.0) for v in pair]


def inside_y(pair):
    rows = pair[1].shape[0]
    return [pair[0], jnp.where(index_of(pair[1].shape, 0) < rows - 1, pair[1], 0.0)]


def rows_of(ref, *at):
    half = ref.shape[-2] // 2
    return [
        jnp.concatenate(
            [
                ref[(*at, v, pl.ds(parity, half, stride=2), slice(None))]
                for v in range(ref.shape[-3])
            ],
            axis=1,
        )
        for parity in range(2)
    ]


def spread_copies(source, stage, sem):
    lead = (slice(None),) * (len(source.shape) - 4)
    return [
        pltpu.make_async_copy(
            source.at[(*lead, tile)], stage.at[(*lead, slice(None), pl.ds(tile * SUBLANES, SUBLANES))], sem
        )
        for tile in range(source.shape[-4])
    ]


def tiled(value):
    *lead, rows, cols = value.shape
    value = value.reshape(*lead, rows // SUBLANES, SUBLANES, cols // LANES, LANES)
    return jnp.swapaxes(value, -2, -3)


def wait_all(stage, sem):
    pltpu.make_async_copy(stage, stage, sem).wait()


def thirds(value):
    high = value.astype(jnp.bfloat16)
    rest = value - high.astype(jnp.float32)
    mid = rest.astype(jnp.bfloat16)
    low = (rest - mid.astype(jnp.float32)).astype(jnp.bfloat16)
    return jnp.concatenate([high, mid, low], axis=1)


def stacked(fields):
    rows = sum(field.shape[0] for field in fields)
    pad = -rows % 16
    if pad:
        fields = list(fields) + [jnp.zeros((pad, fields[0].shape[1]), jnp.float32)]
    return jnp.concatenate(fields, axis=0)


def restrict_pairs(pairs):
    half, cols = pairs[0][0].shape
    sums = stacked([even + odd for even, odd in pairs])
    gather = pair_matrix((2 * LANES, LANES), 0, 0.25).astype(jnp.bfloat16)
    gather = jnp.concatenate([gather] * 3, axis=0)
    merged = jnp.concatenate(
        [
            jnp.dot(thirds(sums[:, c : c + 2 * LANES]), gather, preferred_element_type=jnp.float32)
            for c in range(0, cols, 2 * LANES)
        ],
        axis=1,
    )
    return [merged[i * half : (i + 1) * half] for i in range(len(pairs))]


def prolong_columns(fields):
    half, cols = fields[0].shape
    rows = stacked(fields)
    spread = pair_matrix((LANES, 2 * LANES), 1, 1.0).astype(jnp.bfloat16)
    spread = jnp.concatenate([spread] * 3, axis=0)
    merged = jnp.concatenate(
        [
            jnp.dot(thirds(rows[:, c : c + LANES]), spread, preferred_element_type=jnp.float32)
            for c in range(0, cols, LANES)
        ],
        axis=1,
    )
    return [merged[i * half : (i + 1) * half] for i in range(len(fields))]


def coarse_step(fields, face_x, face_y):
    return power(fields, 1, face_x, face_y)


def power(fields, count, face_x, face_y):
    if count == 0:
        return fields
    s, e, n = fields
    rows, cols = s.shape
    inner_x = index_of(s.shape, 1) < cols - 1
    inner_y = index_of(s.shape, 0) < rows - 1
    e_in, n_in = jnp.where(inner_x, e, 0.0), jnp.where(inner_y, n, 0.0)
    e_edge, n_edge = e - e_in, n - n_in
    face_x = jnp.where(inner_x, face_x, 0.0)
    face_w, face_s = roll(face_x, 1, 1), roll(face_y, 1, 0)

    def body(_, carried):
        s, e, n, west, south = carried
        e = e + face_x * (roll(s, -1, 1) - s)
        n = n + face_y * (roll(s, -1, 0) - s)
        west = west + face_w * (s - roll(s, 1, 1))
        south = south + face_s * (s - roll(s, 1, 0))
        return s + ((e - west) + (n - south)), e, n, west, south

    carried = (s, e_in, n_in, roll(e_in, 1, 1), roll(n_in, 1, 0))
    if count <= 4:
        for step in range(count):
            carried = body(step, carried)
    else:
        carried = lax.fori_loop(0, count, body, carried)
    s, e, n, _, _ = carried
    return s, e + e_edge, n + n_edge


def add(a, b):
    return tuple(x + y for x, y in zip(a, b))


def scaled(a, factor):
    return tuple(x * factor for x in a)


def pick(first, a, b):
    return tuple(jnp.where(first, x, y) for x, y in zip(a, b))


def read(ref, at=0):
    return tuple(ref[at + i] for i in range(3))


def write(ref, fields, at=0):
    for i, field in enumerate(fields):
        ref[at + i] = field


def pair_matrix(shape, wide_axis, weight):
    wide = index_of(shape, wide_axis) // 2
    return jnp.where(wide == index_of(shape, 1 - wide_axis), weight, 0.0)


def product(a, b):
    return jnp.dot(a, b, precision=EXACT, preferred_element_type=jnp.float32)


def prolong_all(fields):
    half, cols = fields[0].shape
    stacked = jnp.concatenate(fields, axis=0)
    stacked = product(pair_matrix((2 * stacked.shape[0], stacked.shape[0]), 0, 1.0), stacked)
    spread = pair_matrix((LANES, 2 * LANES), 1, 1.0)
    merged = jnp.concatenate(
        [product(stacked[:, c : c + LANES], spread) for c in range(0, cols, LANES)], axis=1
    )
    return [merged[2 * i * half : 2 * (i + 1) * half] for i in range(len(fields))]


def prepare(
    table_in,
    levels,
    wet,
    initial,
    forcing,
    velocity,
    own,
    sent,
    planes,
    window_planes,
    coarse_faces,
    stage_f,
    flow,
    table,
    stage_l,
    stage_w,
    stage_i,
    sems,
):
    load_table = pltpu.make_async_copy(table_in, table, sems.at[5])
    load_table.start()
    sources = ((levels, stage_l), (wet, stage_w), (initial.at[0], stage_i), (forcing, stage_f), (velocity, flow))
    for i, (source, stage) in enumerate(sources):
        for copy in spread_copies(source, stage, sems.at[i]):
            copy.start()
    steps = forcing.shape[0]
    width = own.shape[2]
    coarse_cols = stage_l.shape[0] * LANES // 2
    load_table.wait()
    wait_all(stage_l, sems.at[0])
    level = rows_of(stage_l)
    depth = [jnp.zeros(v.shape, jnp.float32) for v in level]
    for i in range(table.shape[0]):
        depth = [jnp.where(v == i, table[i], d) for v, d in zip(level, depth)]
    wait_all(stage_w, sems.at[1])
    dry = [v.astype(jnp.float32) for v in rows_of(stage_w)]
    depth = [d * v for d, v in zip(depth, dry)]
    half = 0.5 * COURANT * COURANT
    face_x = inside_x([half * (d + roll(d, -1, 1)) for d in depth])
    face_y = inside_y([half * (depth[0] + depth[1]), half * (depth[1] + roll(depth[0], -1, 0))])
    all_planes = face_x + face_y + dry
    for i, plane in enumerate(all_planes):
        planes[i] = plane

    wait_all(stage_i, sems.at[2])
    s0 = rows_of(stage_i, 0)
    e0 = [v * COURANT for v in rows_of(stage_i, 1)]
    n0 = [v * COURANT for v in rows_of(stage_i, 2)]
    e_in, n_in = inside_x(e0), inside_y(n0)
    faces_x, faces_y = cut(face_x, face_y)
    s, e, n = cut(s0, e_in, n_in)
    for _ in range(steps):
        s, e, n = fine_step(s, e, n, faces_x, faces_y)
    s, e, n = glued(s, e, n)
    e = [v + (x - y) for v, x, y in zip(e, e0, e_in)]
    n = [v + (x - y) for v, x, y in zip(n, n0, n_in)]
    relaxed = [s, e, n]

    wait_all(stage_f, sems.at[3])
    s = rows_of(stage_f, steps - 1)
    zero = [jnp.zeros_like(v) for v in s]
    s, e, n = cut(s, zero, zero)
    for step in reversed(range(steps - 1)):
        s, e, n = fine_step(
            s, e, n, faces_x, faces_y, forcing=lambda p, v: block_of(stage_f, step, v, parity=p)
        )
    s, e, n = glued(s, e, n)
    for pair, start in zip((s, e, n), (s0, e0, n0)):
        relaxed.append([v - x for v, x in zip(pair, start)])
    su, eu, nu, sw, ew, nw, coarse_depth = restrict_pairs(relaxed + [depth])
    ratio = steps / 2
    coarse_courant = COURANT * ratio
    cx, cy = faces(coarse_depth, coarse_courant * coarse_courant)
    w = (sw, ew * ratio, nw * ratio)
    g = add((su, eu * ratio, nu * ratio), coarse_step(w, cx, cy))

    core = lax.rem(lax.axis_index("tm"), 2)
    right = coarse_cols - width
    window = window_planes.shape[2]

    def store(mine, other, start):
        for i, plane in enumerate(all_planes):
            window_planes[i] = plane[:, start : start + window]
        for ref, at in ((own, mine), (sent, other)):
            for i in range(3):
                ref[i] = g[i][:, at : at + width]
                ref[3 + i] = w[i][:, at : at + width]
        coarse_faces[0] = cx[:, mine : mine + width]
        coarse_faces[1] = cy[:, mine : mine + width]

    @pl.when(core == 0)
    def _():
        store(0, right, 0)

    @pl.when(core == 1)
    def _():
        store(right, 0, 2 * coarse_cols - window)

    wait_all(flow, sems.at[4])


def chip_pair(own, got, coarse_faces, out):
    cx, cy = coarse_faces[0], coarse_faces[1]
    first = lax.rem(lax.axis_index("tm"), 2) == 0
    g_own, g_got = read(own), read(got)
    g_low, g_high = pick(first, g_own, g_got), pick(first, g_got, g_own)
    w_low = pick(first, read(own, 3), read(got, 3))
    write(out, add(g_low, coarse_step(g_high, cx, cy)))
    write(out, add(w_low, g_high), 3)


def row_pair(own, got, coarse_faces, order, out, out_t):
    cx, cy = coarse_faces[0], coarse_faces[1]
    first = lax.rem(lax.axis_index("tm") // 2, 2) == 0
    t_own, t_got = read(own), read(got)
    t_low, t_high = pick(first, t_own, t_got), pick(first, t_got, t_own)
    q_low = pick(first, read(own, 3), read(got, 3))
    moved = coarse_step(t_high, cx, cy)
    total = add(t_low, coarse_step(moved, cx, cy))
    write(out, total)
    write(out_t, total)
    write(out, add(q_low, moved), 3)


def widen(stride, own, got, coarse_faces, out, *, per_row, rows_in_all):
    row = lax.axis_index("tm") // per_row
    there = jnp.where(row + stride < rows_in_all, 1.0, 0.0)
    moved = power(scaled(read(got), there), per_row * stride, coarse_faces[0], coarse_faces[1])
    write(out, add(read(own), moved))


def finish(near, far, farther, own, got, chip, partner, coarse_faces, starts, kept, sent, *, per_row, rows_in_all):
    cx, cy = coarse_faces[0], coarse_faces[1]
    width = coarse_faces.shape[2]
    half = kept.shape[2]
    device = lax.axis_index("tm")
    row = device // per_row

    def there(stride):
        return jnp.where(row + stride < rows_in_all, 1.0, 0.0)

    rest = scaled(read(far), there(2))
    if farther is not None:
        rest = add(rest, power(scaled(read(farther), there(3)), per_row, cx, cy))
    rest = power(rest, per_row - 1, cx, cy)
    after = add(scaled(read(near, 3), there(1)), rest)
    end = add(scaled(read(near), there(1)), coarse_step(rest, cx, cy))
    if partner is not None:
        low = lax.rem(device // 2, 2) == 0
        moved = coarse_step(end, cx, cy)
        after = pick(low, add(read(partner, 3), moved), after)
        end = pick(low, add(read(partner), coarse_step(moved, cx, cy)), end)
    first = lax.rem(device, 2) == 0
    w_high = pick(first, read(got, 3), read(own, 3))
    q = read(chip, 3)
    c_low = add(q, coarse_step(end, cx, cy))
    c_high = add(w_high, end)

    write(starts, pick(first, c_high, after))
    write(starts, pick(first, after, c_high), 3)

    @pl.when(first)
    def _():
        for i in range(3):
            kept[i] = c_low[i][:, :half]
            sent[i] = c_high[i][:, :half]

    @pl.when(jnp.logical_not(first))
    def _():
        for i in range(3):
            kept[i] = c_high[i][:, width - half :]
            sent[i] = c_low[i][:, width - half :]


def joined(kept, got):
    first = lax.rem(lax.axis_index("tm"), 2) == 0
    fields = []
    for i in range(3):
        left = jnp.where(first, kept[i], got[i])
        right = jnp.where(first, got[i], kept[i])
        fields.append(jnp.concatenate([left, right], axis=1))
    return fields


def correct(order, kept, got, initial_in, corrected, done, initial, sem, *, steps):
    load = pltpu.make_async_copy(initial_in, initial, sem)
    load.start()
    done[...] = jnp.zeros_like(done)
    unscale = 1.0 / (COURANT * (steps / 2))
    s, e, n = joined(kept, got)
    fields = prolong_all([s, e * unscale, n * unscale])
    load.wait()
    for i, field in enumerate(fields):
        corrected[0, i] = initial[0, i] + field


def pulled(slopes, dry):
    grad_x, grad_y = inside_x(slopes[0]), inside_y(slopes[1])
    across = [grad_y[0] + roll(grad_y[1], 1, 0), grad_y[1] + grad_y[0]]
    return [
        (0.5 * COURANT) * ((x + roll(x, 1, 1)) + y) * keep for x, y, keep in zip(grad_x, across, dry)
    ]


def base(order, following, stage_f, flow, planes, mine, other, stage_i, sem):
    for copy in spread_copies(following.at[0], stage_i, sem):
        copy.start()
    steps = flow.shape[0]
    device = lax.axis_index("tm")
    there = jnp.where(device + 1 < lax.axis_size("tm"), 1.0, 0.0)
    face_x, face_y = [planes[0], planes[1]], [planes[2], planes[3]]
    wait_all(stage_i, sem)
    s = [v * there for v in rows_of(stage_i, 0)]
    e = inside_x([v * (there * COURANT) for v in rows_of(stage_i, 1)])
    n = inside_y([v * (there * COURANT) for v in rows_of(stage_i, 2)])
    s, e, n, faces_x, faces_y = cut(s, e, n, face_x, face_y)
    sums = [[[], []], [[], []]]
    for step in reversed(range(steps)):
        s, e, n = fine_step(
            s,
            e,
            n,
            faces_x,
            faces_y,
            forcing=lambda p, v: block_of(stage_f, step, v, parity=p),
            flow=lambda k, p, v: block_of(flow, step, k, v, parity=p),
            sums=sums,
        )
    sums = glued(*sums)
    total = pulled(sums, [planes[4], planes[5]])
    first = lax.rem(device, 2) == 0
    half = mine.shape[2]

    @pl.when(first)
    def _():
        for i in range(2):
            mine[i] = total[i][:, :half]
            other[i] = total[i][:, half:]

    @pl.when(jnp.logical_not(first))
    def _():
        for i in range(2):
            mine[i] = total[i][:, half:]
            other[i] = total[i][:, :half]


def cut_flow(order, velocity, out, sem):
    blocks = out.shape[2]
    start = lax.rem(lax.axis_index("tm"), 2) * (velocity.shape[3] - blocks)
    for copy in spread_copies(velocity.at[:, :, :, pl.ds(start, blocks)], out, sem):
        copy.start()
    wait_all(out, sem)


def descend(starts, flow, flow_got, planes, grad, grad_got, mine):
    steps = flow.shape[0]
    half = mine.shape[2]
    width = starts.shape[2]
    window = planes.shape[2]
    first = lax.rem(lax.axis_index("tm"), 2) == 0
    inverse = 1.0 / (steps / 2)
    shift = width - window // 2
    fields = [jnp.where(first, starts[i], roll(starts[i], -shift, 1)) for i in range(6)]
    fields = [field[:, :window] for field in prolong_columns(fields)]
    face_x, face_y = inside_x([planes[0], planes[1]]), [planes[2], planes[3]]
    sums = [[[], []], [[], []]]
    start = jnp.where(first, 0, flow.shape[2] - flow_got.shape[2])
    faces_x, faces_y = cut(face_x, face_y)
    for i, (velocity, at) in enumerate(((flow, start), (flow_got, 0))):
        s, e, n = fields[3 * i : 3 * i + 3]
        e, n = e * inverse, n * inverse
        s, e, n = cut([s, s], inside_x([e, e]), inside_y([n, n]))
        for step in reversed(range(steps)):
            s, e, n = fine_step(
                s,
                e,
                n,
                faces_x,
                faces_y,
                flow=lambda k, p, v: block_of(velocity, step, k, at + v, parity=p),
                sums=sums,
            )
    total = glued(*sums)
    total = pulled(total, [planes[4], planes[5]])
    for i in range(2):
        valid = jnp.where(first, total[i][:, :half], total[i][:, window - half :])
        mine[i] = valid + (grad[i] + grad_got[i])


def plus(a, b, order, out):
    out[...] = a[...] + b[...]


def plus_all(a, b, c, d, order, out):
    out[...] = (a[...] + b[...]) + (c[...] + d[...])


def weave(mine, other, out, stage, sem):
    first = lax.rem(lax.axis_index("tm"), 2) == 0
    half = stage.shape[1] // 2
    blocks = stage.shape[0] // 2
    for i in range(2):
        left, right = jnp.where(first, mine[i], other[i]), jnp.where(first, other[i], mine[i])
        for v in range(blocks):
            at = slice(v * LANES, (v + 1) * LANES)
            stage[v, pl.ds(i, half, stride=2), :] = left[:, at]
            stage[blocks + v, pl.ds(i, half, stride=2), :] = right[:, at]
    for tile in range(out.shape[0]):
        rows = pl.ds(tile * SUBLANES, SUBLANES)
        pltpu.make_async_copy(stage.at[:, rows], out.at[tile], sem).start()
    wait_all(stage, sem)


def call(body, shapes, operands, *, specs=None, outs=None, scratch=(), cost=1000):
    return pl.pallas_call(
        body,
        out_shape=[jax.ShapeDtypeStruct(shape, jnp.float32) for shape in shapes],
        in_specs=specs or [VMEM] * len(operands),
        out_specs=outs or [VMEM] * len(shapes),
        scratch_shapes=scratch,
        cost_estimate=pl.CostEstimate(flops=cost, bytes_accessed=cost, transcendentals=0),
        compiler_params=pltpu.CompilerParams(vmem_limit_bytes=32 * 1024 * 1024),
    )(*operands)


def in_hbm(value):
    return pltpu.with_memory_space_constraint(value, pltpu.HBM)


def shards(initial, velocity, forcing, depth_table, levels, wet_mask):
    count = lax.axis_size("tm")
    rows, cols = levels.shape
    steps = forcing.shape[0]
    half_rows, half = rows // 2, cols // 4
    halo = -(-count // LANES) * LANES
    width = half + halo
    block = (half_rows, width)
    blocks = cols // LANES
    window = cols // 2 - (-(steps + 1) // LANES) * LANES
    plane = (half_rows, cols)

    def paired(value, stride):
        return lax.ppermute(value, "tm", [(s, s ^ stride) for s in range(count)])

    def back(value, stride):
        return lax.ppermute(value, "tm", [(s, (s - stride) % count) for s in range(count)])

    def stage(*lead, kind=jnp.float32):
        return pltpu.VMEM((*lead, blocks, rows, LANES), kind)

    tiled_in = dict(levels=levels, wet=wet_mask, initial=initial, forcing=forcing, velocity=velocity)
    tiled_in = {name: in_hbm(tiled(value)) for name, value in tiled_in.items()}
    pinned = in_hbm(initial)
    velocity_got = paired(velocity, 1)
    following = lax.ppermute(initial, "tm", [(s, s - 1) for s in range(1, count)])
    own, sent, planes, window_planes, coarse_faces, staged_forcing, flow = call(
        prepare,
        [
            (6, *block),
            (6, *block),
            (6, *plane),
            (6, half_rows, window),
            (2, *block),
            (steps, blocks, rows, LANES),
            (steps, 2, blocks, rows, LANES),
        ],
        [in_hbm(depth_table), *(tiled_in[name] for name in ("levels", "wet", "initial", "forcing", "velocity"))],
        specs=[HBM] * 6,
        scratch=[
            pltpu.SMEM(depth_table.shape, jnp.float32),
            stage(kind=jnp.int32),
            stage(kind=jnp.int32),
            stage(3),
            pltpu.SemaphoreType.DMA((6,)),
        ],
        cost=PREPARE_COST,
    )
    got = paired(sent, 1)
    (chip,) = call(
        chip_pair, [(6, *block)], [own, got, coarse_faces]
    )
    grad, grad_other = call(
        base,
        [(2, half_rows, cols // 2)] * 2,
        [chip, tiled(following), staged_forcing, flow, planes],
        specs=[ANY] + [VMEM] * 4,
        scratch=[stage(3), pltpu.SemaphoreType.DMA],
        cost=BASE_COST,
    )
    grad_got = paired(grad_other, 1)
    per_row = 4 if count <= 16 else 2
    rows_in_all = count // per_row
    if per_row == 4:
        partner = paired(chip, 2)
        row, row_t = call(
            row_pair,
            [(6, *block), (3, *block)],
            [chip, partner, coarse_faces, grad_got],
            specs=[VMEM] * 3 + [ANY],
        )
    else:
        partner = None
        row, row_t = chip, chip[:3]
    near = back(row, per_row)
    if rows_in_all <= 4:
        far, farther = back(row_t, 2 * per_row), back(row_t, 3 * per_row)
    else:
        stride = 1
        while stride < rows_in_all - 2:
            (row_t,) = call(
                functools.partial(widen, stride, per_row=per_row, rows_in_all=rows_in_all),
                [(3, *block)],
                [row_t, back(row_t, stride * per_row), coarse_faces],
            )
            stride *= 2
        far, farther = back(row_t, 2 * per_row), None

    (flow_got,) = call(
        cut_flow,
        [(steps, 2, window // LANES, rows, LANES)],
        [row_t, tiled(velocity_got)],
        specs=[ANY, ANY],
        scratch=[pltpu.SemaphoreType.DMA],
        cost=SPLIT_COST,
    )

    operands = {
        "near": near,
        "far": far,
        "farther": farther,
        "own": own,
        "got": got,
        "chip": chip,
        "partner": partner,
        "coarse_faces": coarse_faces,
    }
    names = [name for name, value in operands.items() if value is not None]

    def finish_body(*refs):
        given = dict.fromkeys(operands)
        given.update(zip(names, refs))
        starts, kept, sent = refs[len(names) + 1 :]
        finish(**given, starts=starts, kept=kept, sent=sent, per_row=per_row, rows_in_all=rows_in_all)

    starts, kept, sent = call(
        finish_body,
        [(6, *block), (3, half_rows, half), (3, half_rows, half)],
        [operands[name] for name in names] + [flow_got],
        specs=[VMEM] * len(names) + [ANY],
    )
    (mine,) = call(
        descend,
        [(2, half_rows, cols // 2)],
        [starts, flow, flow_got, window_planes, grad, grad_got],
        cost=BASE_COST,
    )
    got = paired(sent, 1)
    if per_row == 4:
        (mine,) = call(plus, [mine.shape], [mine, paired(mine, 2), got], specs=[VMEM, VMEM, ANY])
    corrected, done = call(
        functools.partial(correct, steps=steps),
        [initial.shape, (8, LANES)],
        [mine, kept, got, pinned],
        specs=[ANY, VMEM, VMEM, HBM],
        scratch=[pltpu.VMEM(initial.shape, jnp.float32), pltpu.SemaphoreType.DMA],
        cost=CORRECT_COST,
    )
    if rows_in_all == 4:
        parts = [mine] + [paired(mine, stride) for stride in (4, 8, 12)]
        (mine,) = call(plus_all, [mine.shape], parts + [done], specs=[VMEM] * 4 + [ANY])
    else:
        stride = per_row
        while stride < count:
            mine = mine + paired(mine, stride)
            stride *= 2
    (gradient,) = call(
        weave,
        [(rows // SUBLANES, blocks, SUBLANES, LANES)],
        [mine, paired(mine, 1)],
        outs=[HBM],
        scratch=[stage(), pltpu.SemaphoreType.DMA],
    )
    return corrected, jnp.swapaxes(gradient, 1, 2).reshape(rows, cols)


def solution(mesh):
    in_specs = (
        P("tm", "parts", None, None),
        P("tm", "parts", None, None),
        P("tm", "parts", None),
        P(),
        P("parts", None),
        P("parts", None),
    )
    out_specs = (P("tm", "parts", None, None), P("parts", None))
    return jax.shard_map(shards, mesh=mesh, in_specs=in_specs, out_specs=out_specs, check_vma=False)
```
